32 devices in a mesh: ctx: 8 (over y, x, core), tp: 4 (over z).
Axes of the slice: x: 2, y: 2, z: 4, core: 2. Of those that a mesh axis runs over, the one named last changes fastest.
Arguments:
- main_q: bfloat16 [3584, 24576], P('ctx', 'tp'), may hold values from -6 to 6
- main_k: bfloat16 [1024, 24576], P('ctx', 'tp'), may hold values from -6 to 6
- log_norms: float32 [3584, 128], P('ctx', 'tp'), may hold values from 0 to 4
- index_q: bfloat16 [3584, 64, 128], P(('ctx', 'tp')), may hold values from -8 to 8
- index_w: float32 [3584, 64], P(('ctx', 'tp')), may hold values from -2 to 2
- index_k: bfloat16 [1024, 128], P('ctx'), may hold values from -8 to 8
- row_weight: float32 [3584], P(('ctx', 'tp')), may hold values from 10 to 200
- offsets: int32 [8], P('ctx'), may hold values from 0 to 576
- key_map: int32 [8], replicated, may hold values from 0 to 7, as said below
Outputs:
- grad_index_q: float32 [3584, 64, 128], P(('ctx', 'tp'))
- grad_index_w: float32 [3584, 64], P(('ctx', 'tp'))
- grad_index_k: float32 [1024, 128], P(('ctx', 'tp'))
The draws below stay inside these ranges and needn't reach their ends.
Inputs may be any that keep to these rules, and one draw needn't show every extreme that they name: `key_map`: each key block number appears exactly once.
All inputs are finite; a program needn't handle non-finite values.
Results may differ from the reference program's by a relative error of at most 0.0028.
Values may be sent and summed in bfloat16 or wider, within the bound.
No kernel may reach another device: no remote copies, remote signals or barrier semaphores. Data moves between devices by JAX's collectives and lax.ppermute only.
A program may use at most 128 MiB of HBM per device.

```python
import math
import jax
import jax.numpy as jnp
from jax import lax

H = 128
DQK = 192
HI = 64
DI = 128
Q_DEV = 448
KEY_DEV = 128
BLOCKS = 8
QUERIES = 3584
KEYS = 1024
N_TP = 4


def drawn_normal(key, shape, limit):
    return jnp.clip(jax.random.normal(key, shape, jnp.float32), -limit, limit)


def row_scales(key, count, low, high):
    return jnp.exp(jax.random.uniform(key, (count, 1), jnp.float32, math.log(low), math.log(high)))


def main_values(key, count):
    common = drawn_normal(jax.random.fold_in(key, 1), (count, 1, DQK), 4.0)
    own = drawn_normal(jax.random.fold_in(key, 2), (count, H, DQK), 4.0)
    values = 1.41 * common + 0.71 * own
    return jnp.clip(values, -6.0, 6.0).reshape(count, H * DQK)


def draw_main_q(key, part):
    return main_values(jax.random.fold_in(key, 21), QUERIES).astype(jnp.bfloat16)


def draw_main_k(key, part):
    return main_values(jax.random.fold_in(key, 22), KEYS).astype(jnp.bfloat16)


def indexer_parts(key):
    key_map = jax.random.permutation(jax.random.fold_in(key, 11), BLOCKS).astype(jnp.int32)
    weights = 0.3 * drawn_normal(jax.random.fold_in(key, 12), (QUERIES, HI), 4.0)
    key_noise = drawn_normal(jax.random.fold_in(key, 13), (KEYS, DI), 4.0)
    query_noise = drawn_normal(jax.random.fold_in(key, 14), (QUERIES, HI, DI), 4.0)
    index_k = key_noise * row_scales(jax.random.fold_in(key, 17), KEYS, 0.25, 2.5)
    index_q = query_noise * row_scales(jax.random.fold_in(key, 18), QUERIES, 0.4, 1.2)[:, :, None]
    index_q = jnp.clip(index_q, -8.0, 8.0)
    index_k = jnp.clip(index_k, -8.0, 8.0)
    weights = jnp.clip(weights, -2.0, 2.0)
    return (key_map, index_q, index_k, weights)


def draw_key_map(key, part):
    return indexer_parts(key)[0]


def draw_index_q(key, part):
    return indexer_parts(key)[1].astype(jnp.bfloat16)


def draw_index_k(key, part):
    return indexer_parts(key)[2].astype(jnp.bfloat16)


def draw_index_w(key, part):
    return indexer_parts(key)[3]


def plant(drawn, stream_key, least, top_value):
    longest = drawn.shape.index(max(drawn.shape))
    spots = []
    for shift in (0, 1):
        where = [jax.random.randint(jax.random.fold_in(stream_key, axis), (), 0, length) for axis, length in enumerate(drawn.shape)]
        where[longest] = (where[longest] + shift) % drawn.shape[longest]
        spots.append(tuple(where))
    return drawn.at[spots[0]].set(least).at[spots[1]].set(top_value)


def level_of(stream_key, dims, pieces, least, largest):
    factor_of, own = 1.0, jax.random.fold_in(stream_key, 6)
    for dim, blocks in pieces:
        steps = jnp.exp(jax.random.uniform(jax.random.fold_in(own, dim), (blocks,), jnp.float32, least / len(pieces), largest / len(pieces)))
        factor_of = factor_of * jnp.repeat(steps, dims[dim] // blocks).reshape([-1 if axis == dim else 1 for axis in range(len(dims))])
    return factor_of


def setup_inputs(seed: int = 0) -> dict:
    arg_keys = jax.random.split(jax.random.key(seed), 10)
    main_q = draw_main_q(jax.random.fold_in(arg_keys[9], 71), 0)
    main_k = draw_main_k(jax.random.fold_in(arg_keys[9], 71), 0)
    log_norms = jnp.clip(4.0 * jax.random.uniform(arg_keys[2], (QUERIES, H), jnp.float32) ** level_of(arg_keys[2], (QUERIES, H), ((0, 8), (1, 4)), -0.2, 0.2), 0.0, 4.0)
    index_q = draw_index_q(jax.random.fold_in(arg_keys[9], 71), 0)
    index_w = draw_index_w(jax.random.fold_in(arg_keys[9], 71), 0)
    index_k = draw_index_k(jax.random.fold_in(arg_keys[9], 71), 0)
    row_weight = jnp.clip(jnp.exp(math.log(200.0) - 2.9957323 * jax.random.uniform(arg_keys[6], (QUERIES,), jnp.float32) ** level_of(arg_keys[6], (QUERIES,), ((0, 32),), -0.2, 0.2)), 10.0, 200.0)
    offsets = plant(jax.random.randint(arg_keys[7], (BLOCKS,), 0, KEYS - Q_DEV + 1), jax.random.fold_in(arg_keys[7], 1), 0, KEYS - Q_DEV).astype(jnp.int32)
    key_map = draw_key_map(jax.random.fold_in(arg_keys[9], 71), 0)
    return {"main_q": main_q, "main_k": main_k, "log_norms": log_norms, "index_q": index_q, "index_w": index_w, "index_k": index_k, "row_weight": row_weight, "offsets": offsets, "key_map": key_map}


def reference(main_q, main_k, log_norms, index_q, index_w, index_k, row_weight, offsets, key_map):
    own_rows = Q_DEV // N_TP
    block_count = QUERIES // own_rows
    storage = jnp.arange(KEYS, dtype=jnp.int32)
    key_pos = key_map[storage // KEY_DEV] * KEY_DEV + storage % KEY_DEV
    query_rows = jnp.arange(QUERIES, dtype=jnp.int32)
    query_pos = offsets[query_rows // Q_DEV] + query_rows % Q_DEV
    keys_wide = main_k.astype(jnp.float32).reshape(KEYS, H, DQK)
    index_keys = index_k.astype(jnp.float32)
    score_scale = 1.0 / math.sqrt(DQK)
    inv_root = 1.0 / math.sqrt(DI)

    def one_block(running, number):
        first_row = (number * own_rows).astype(jnp.int32)
        queries = lax.dynamic_slice_in_dim(main_q, first_row, own_rows, 0).astype(jnp.float32).reshape(own_rows, H, DQK)
        norm_rows = lax.dynamic_slice_in_dim(log_norms, first_row, own_rows, 0)
        row_pos = lax.dynamic_slice_in_dim(query_pos, first_row, own_rows, 0)
        visible = key_pos[None, :] <= row_pos[:, None]
        scores = jnp.einsum('qhd,khd->qhk', queries, keys_wide) * score_scale
        prob_terms = jnp.where(visible[:, None, :], jnp.exp(scores - norm_rows[:, :, None]), 0.0)
        head_mass = lax.optimization_barrier(jnp.sum(prob_terms, axis=1))
        target = head_mass / lax.optimization_barrier(jnp.sum(head_mass, axis=1, keepdims=True))
        index_rows = lax.dynamic_slice_in_dim(index_q, first_row, own_rows, 0).astype(jnp.float32)
        weight_rows = lax.dynamic_slice_in_dim(index_w, first_row, own_rows, 0)
        loss_rows = lax.dynamic_slice_in_dim(row_weight, first_row, own_rows, 0)
        inner = jnp.einsum('tjd,kd->tjk', index_rows, index_keys) * inv_root
        logits = lax.optimization_barrier(jnp.sum(weight_rows[:, :, None] * jax.nn.softplus(inner), axis=1))
        masked = jnp.where(visible, logits, -jnp.inf)
        row_max = lax.optimization_barrier(jnp.max(masked, axis=1, keepdims=True))
        exp_terms = jnp.exp(masked - row_max)
        index_probs = exp_terms / lax.optimization_barrier(jnp.sum(exp_terms, axis=1, keepdims=True))
        logit_grad = loss_rows[:, None] * (index_probs - target)
        grad_w = lax.optimization_barrier(jnp.sum(logit_grad[:, None, :] * jax.nn.softplus(inner), axis=2))
        score_grad = (logit_grad[:, None, :] * weight_rows[:, :, None] * jax.nn.sigmoid(inner) * inv_root).astype(jnp.bfloat16)
        score_wide = score_grad.astype(jnp.float32)
        grad_q = jnp.einsum('tjk,kd->tjd', score_wide, index_keys)
        running = running + jnp.einsum('tjk,tjd->kd', score_wide, index_rows)
        return (running, (grad_q, grad_w))
    grad_k, stacked = lax.scan(one_block, jnp.zeros((KEYS, DI), jnp.float32), jnp.arange(block_count, dtype=jnp.int32))
    grad_q = stacked[0].reshape(QUERIES, HI, DI)
    grad_w = stacked[1].reshape(QUERIES, HI)
    return (grad_q, grad_w, grad_k)
```

```python
import functools
import math

import jax
import jax.numpy as jnp
from jax import lax
from jax.experimental import pallas as pl
from jax.experimental.pallas import tpu as pltpu
from jax.sharding import PartitionSpec as P

LOG2E = math.log2(math.e)
LN2 = math.log(2.0)
VMEM_BYTES = 56 * 1024 * 1024
BF = jnp.bfloat16
F32 = jnp.float32


def prep_kernel(width, heads_step, root, q_ref, ln_ref, out_ref):
    step = pl.program_id(0)
    heads = ln_ref.shape[1]
    pad = 2 * 128
    cols = heads_step * pad
    scaled = -root * ln_ref[...]
    high = scaled.astype(BF)
    rest = scaled - high.astype(F32)
    mid = rest.astype(BF)
    low = (rest - mid.astype(F32)).astype(BF)
    column = lax.broadcasted_iota(jnp.int32, (heads, cols), 1)
    head = lax.broadcasted_iota(jnp.int32, (heads, cols), 0) - step * heads_step
    spare = jnp.where(head % 2 == 0, width, 0)
    offset = column - head * pad - spare
    extra = jnp.zeros((q_ref.shape[0], cols), F32)
    for number, piece in enumerate((high, mid, low)):
        place = jnp.where(offset == number, 1.0, 0.0).astype(BF)
        extra = extra + jnp.dot(piece, place, preferred_element_type=F32)
    lane = lax.broadcasted_iota(jnp.int32, (q_ref.shape[0], pad), 1)
    for h in range(heads_step):
        first = (h // 2) * 2 * width + (h % 2) * (2 * width - pad)
        kept = lane < width if h % 2 == 0 else lane >= pad - width
        own = q_ref[:, first : first + pad].astype(F32)
        out_ref[:, h * pad : (h + 1) * pad] = jnp.where(
            kept, own, extra[:, h * pad : (h + 1) * pad]
        ).astype(BF)


def prep(main_q, log_norms, width):
    rows, total = main_q.shape
    heads = log_norms.shape[1]
    step_heads = 8
    return pl.pallas_call(
        functools.partial(prep_kernel, width, step_heads, math.sqrt(width)),
        grid=(heads // step_heads,),
        in_specs=[
            pl.BlockSpec((rows, step_heads * width), lambda i: (0, i)),
            pl.BlockSpec((rows, heads), lambda i: (0, 0)),
        ],
        out_specs=pl.BlockSpec((rows, step_heads * 256), lambda i: (0, i)),
        out_shape=jax.ShapeDtypeStruct((rows, heads * 256), BF),
        compiler_params=pltpu.CompilerParams(vmem_limit_bytes=VMEM_BYTES),
        name="prep",
    )(main_q, log_norms)


def mass_kernel(width, heads_step, n_keys, ranks, pos_ref, qa_ref, kpos_ref, *refs):
    key_refs, out_refs, total_ref = refs[:n_keys], refs[n_keys : n_keys + ranks], refs[n_keys + ranks]
    step = pl.program_id(0)
    pad = 256
    factor = LOG2E / math.sqrt(width)
    total = sum(r.shape[0] for r in key_refs)
    lane = lax.broadcasted_iota(jnp.int32, (total, pad), 1)
    ones_even = jnp.where((lane >= width) & (lane < width + 3), 1.0, 0.0).astype(BF)
    ones_odd = jnp.where(lane < 3, 1.0, 0.0).astype(BF)
    keep_even = jnp.where(lane < width, 1.0, 0.0).astype(BF)
    keep_odd = jnp.where(lane >= pad - width, 1.0, 0.0).astype(BF)

    @pl.when(step == 0)
    def _():
        total_ref[...] = jnp.zeros_like(total_ref)

    def one(h):
        first = (h // 2) * 2 * width + (h % 2) * (2 * width - pad)
        parts = [r[:, first : first + pad] for r in key_refs]
        keys = parts[0] if len(parts) == 1 else jnp.concatenate(parts, axis=0)
        if h % 2 == 0:
            keys = keys * keep_even + ones_even
        else:
            keys = keys * keep_odd + ones_odd
        scores = lax.dot_general(
            qa_ref[:, h * pad : (h + 1) * pad], keys, (((1,), (1,)), ((), ())),
            preferred_element_type=F32,
        )
        return jnp.exp2(scores * factor)

    for h in range(0, heads_step, 2):
        total_ref[...] += one(h) + one(h + 1)

    @pl.when(step == pl.num_programs(0) - 1)
    def _():
        own = total_ref.shape[0] // ranks
        for k in range(ranks):
            first = lax.rem(pos_ref[1] + k, ranks) * own
            row = pos_ref[0] + first + lax.broadcasted_iota(jnp.int32, out_refs[k].shape, 0)
            rows = total_ref[pl.ds(pl.multiple_of(first, 8), own), :]
            out_refs[k][...] = jnp.where(kpos_ref[...] <= row, rows, 0.0)


def mass(places, qa, kpos, key_list, width, ranks, step_heads=8):
    rows = qa.shape[0]
    heads = qa.shape[1] // 256
    total = sum(k.shape[0] for k in key_list)
    own = rows // ranks
    return pl.pallas_call(
        functools.partial(mass_kernel, width, step_heads, len(key_list), ranks),
        grid=(heads // step_heads,),
        in_specs=[
            pl.BlockSpec(memory_space=pltpu.SMEM),
            pl.BlockSpec((rows, step_heads * 256), lambda i: (0, i)),
            pl.BlockSpec((1, total), lambda i: (0, 0)),
        ]
        + [pl.BlockSpec((k.shape[0], step_heads * width), lambda i: (0, i)) for k in key_list],
        out_specs=[pl.BlockSpec((own, total), lambda i: (0, 0))] * ranks,
        out_shape=[jax.ShapeDtypeStruct((own, total), F32)] * ranks,
        scratch_shapes=[pltpu.VMEM((rows, total), F32)],
        compiler_params=pltpu.CompilerParams(vmem_limit_bytes=VMEM_BYTES),
        name="mass",
    )(places, qa, kpos, *key_list)


def first_kernel(heads, rows, scale, pos_ref, q_ref, key_ref, w_ref, kpos_ref,
                 sig_ref, dev_ref, prob_ref, raw, soft):
    keys = key_ref.shape[0]
    raw[...] = lax.dot_general(
        q_ref[...], key_ref[...], (((1,), (1,)), ((), ())), preferred_element_type=F32
    )
    w_turned = jnp.transpose(w_ref[...])
    for t in range(rows):
        w = w_turned[:, t : t + 1]
        w_soft = w * LN2
        w_sig = w * scale
        for c in range(keys // 128):
            at = (slice(t * heads, (t + 1) * heads), slice(c * 128, (c + 1) * 128))
            u = raw[at] * (scale * LOG2E)
            low = jnp.minimum(u, 0.0)
            high = jnp.maximum(u, 0.0)
            e = jnp.exp2(low - high)
            log_term = jnp.where(e < 2.0**-11, e * LOG2E, jnp.log2(1.0 + e))
            sp = high + log_term
            soft[at] = sp
            sig_ref[at] = jnp.exp2(low - log_term) * w_sig
            prob_ref[t : t + 1, c * 128 : (c + 1) * 128] = jnp.sum(w_soft * sp, axis=0, keepdims=True)

    row = pos_ref[0] + pl.program_id(0) * rows + lax.broadcasted_iota(jnp.int32, prob_ref.shape, 0)
    masked = jnp.where(kpos_ref[...] <= row, prob_ref[...], -jnp.inf)
    top = jnp.max(masked, axis=1, keepdims=True)
    terms = jnp.exp2((masked - top) * LOG2E)
    prob_ref[...] = terms / jnp.sum(terms, axis=1, keepdims=True)

    for t in range(rows):
        total = jnp.zeros((heads, 128), F32)
        for c in range(keys // 128):
            at = (slice(t * heads, (t + 1) * heads), slice(c * 128, (c + 1) * 128))
            total = total + soft[at] * prob_ref[t : t + 1, c * 128 : (c + 1) * 128]
        mean = LN2 * jnp.sum(total, axis=1, keepdims=True)
        for c in range(keys // 128):
            at = (slice(t * heads, (t + 1) * heads), slice(c * 128, (c + 1) * 128))
            dev_ref[at] = (mean - LN2 * soft[at]).astype(BF)


def first_pass(own_pos, q_flat, keys, weights, kpos, rows=8):
    total, width = q_flat.shape
    key_total = keys.shape[0]
    own, heads = weights.shape
    tile = rows * heads
    return pl.pallas_call(
        functools.partial(first_kernel, heads, rows, 1.0 / math.sqrt(width)),
        grid=(own // rows,),
        in_specs=[
            pl.BlockSpec(memory_space=pltpu.SMEM),
            pl.BlockSpec((tile, width), lambda i: (i, 0)),
            pl.BlockSpec((key_total, width), lambda i: (0, 0)),
            pl.BlockSpec((rows, heads), lambda i: (i, 0)),
            pl.BlockSpec((1, key_total), lambda i: (0, 0)),
        ],
        out_specs=[
            pl.BlockSpec((tile, key_total), lambda i: (i, 0)),
            pl.BlockSpec((tile, key_total), lambda i: (i, 0)),
            pl.BlockSpec((rows, key_total), lambda i: (i, 0)),
        ],
        out_shape=[
            jax.ShapeDtypeStruct((total, key_total), F32),
            jax.ShapeDtypeStruct((total, key_total), BF),
            jax.ShapeDtypeStruct((own, key_total), F32),
        ],
        scratch_shapes=[pltpu.VMEM((tile, key_total), F32), pltpu.VMEM((tile, key_total), F32)],
        compiler_params=pltpu.CompilerParams(vmem_limit_bytes=VMEM_BYTES),
        name="first_pass",
    )(own_pos, q_flat, keys, weights, kpos)


def second_kernel(heads, rows, group, splits, sig_ref, dev_ref, prob_ref, rw_ref, key_ref, qt_ref, *refs):
    count = sum(splits)
    parts, (gq_ref, gw_ref, gk_ref, grad, sums) = refs[:count], refs[count:]
    keys = key_ref.shape[0]
    groups = []
    for size in splits:
        groups.append(sum(r[...] for r in parts[:size]))
        parts = parts[size:]
    mass_rows = jnp.concatenate(groups, axis=1)
    target = rw_ref[...] * mass_rows / jnp.sum(mass_rows, axis=1, keepdims=True)
    coef = rw_ref[...] * prob_ref[...] - target

    @pl.when(pl.program_id(0) == 0)
    def _():
        gk_ref[...] = jnp.zeros_like(gk_ref)

    span = group * heads
    for g in range(rows // group):
        for u in range(group):
            t = g * group + u
            total = jnp.zeros((heads, 128), F32)
            for c in range(keys // 128):
                at = (slice(t * heads, (t + 1) * heads), slice(c * 128, (c + 1) * 128))
                cols = slice(c * 128, (c + 1) * 128)
                grad[at] = (sig_ref[at] * coef[t : t + 1, cols]).astype(BF)
                total = total + dev_ref[at].astype(F32) * target[t : t + 1, cols]
            sums[t * heads : (t + 1) * heads, :] = total
        block = grad[g * span : (g + 1) * span, :]
        gq_ref[g * span : (g + 1) * span, :] = jnp.dot(block, key_ref[...], preferred_element_type=F32)
        gk_ref[...] += jnp.dot(qt_ref[:, g * span : (g + 1) * span], block, preferred_element_type=F32)
    ones = jnp.ones((8, 128), F32)
    added = lax.dot_general(
        ones, sums[...], (((1,), (1,)), ((), ())), preferred_element_type=F32, precision=lax.Precision.HIGHEST
    )
    gw_ref[...] = added.reshape(gw_ref.shape)


def second_pass(sig, dev, prob, mass_parts, row_weight, keys, q_turned, heads, rows=8, group=4):
    total, key_total = sig.shape
    own = total // heads
    tile = rows * heads
    width = keys.shape[1]
    flat = [piece for pieces in mass_parts for piece in pieces]
    gq, gw, gk = pl.pallas_call(
        functools.partial(second_kernel, heads, rows, group, tuple(len(p) for p in mass_parts)),
        grid=(own // rows,),
        in_specs=[
            pl.BlockSpec((tile, key_total), lambda i: (i, 0)),
            pl.BlockSpec((tile, key_total), lambda i: (i, 0)),
            pl.BlockSpec((rows, key_total), lambda i: (i, 0)),
            pl.BlockSpec((rows, 1), lambda i: (i, 0)),
            pl.BlockSpec((key_total, width), lambda i: (0, 0)),
            pl.BlockSpec((width, tile), lambda i: (0, i)),
        ]
        + [pl.BlockSpec((rows, p.shape[1]), lambda i: (i, 0)) for p in flat],
        out_specs=[
            pl.BlockSpec((tile, width), lambda i: (i, 0)),
            pl.BlockSpec((1, 8, tile), lambda i: (i, 0, 0)),
            pl.BlockSpec((width, key_total), lambda i: (0, 0)),
        ],
        out_shape=[
            jax.ShapeDtypeStruct((total, width), F32),
            jax.ShapeDtypeStruct((own // rows, 8, tile), F32),
            jax.ShapeDtypeStruct((width, key_total), F32),
        ],
        scratch_shapes=[pltpu.VMEM((tile, key_total), BF), pltpu.VMEM((tile, 128), F32)],
        compiler_params=pltpu.CompilerParams(vmem_limit_bytes=VMEM_BYTES),
        name="second_pass",
    )(sig, dev, prob, row_weight, keys, q_turned, *flat)
    return gq, gw[:, 0, :].reshape(own, heads), gk


def swap(x, bit):
    size = lax.axis_size("ctx")
    return lax.ppermute(x, "ctx", [(i, i ^ bit) for i in range(size)])


def turn(x, steps):
    size = lax.axis_size("tp")
    return lax.ppermute(x, "tp", [(i, (i + steps) % size) for i in range(size)])


def after(x, *others):
    return lax.optimization_barrier((x, *others))[0]


def per_device(main_q, main_k, log_norms, index_q, index_w, index_k, row_weight, offsets, key_map):
    key_rows = main_k.shape[0]
    own_rows, heads, index_width = index_q.shape
    main_heads = log_norms.shape[1]
    width = main_k.shape[1] // main_heads
    places_ctx = lax.axis_size("ctx")
    ranks = lax.axis_size("tp")
    here = lax.axis_index("ctx")
    rank = lax.axis_index("tp")
    half = key_rows // 2
    far_bits = [b for b in (2**i for i in range(1, places_ctx.bit_length() - 1))]
    far = [sum(b for i, b in enumerate(far_bits) if n >> i & 1) for n in range(1, 2 ** len(far_bits))]
    near_far = [d for d in far if d & (d - 1) == 0]
    rest_far = [d for d in far if d & (d - 1) != 0]

    top, low = main_k[:half], main_k[half:]
    pieces = {(0, 0): top, (0, 1): low}
    index_keys = swap(index_k, 1)
    index_keys = jnp.concatenate([index_k, index_keys], axis=0)
    for n, b in enumerate(near_far):
        for part in (1 - n % 2, n % 2):
            pieces[b, part] = swap(pieces[0, part], b)
    sibling = swap(main_k, 1)
    for b in far_bits:
        index_keys = jnp.concatenate([index_keys, swap(index_keys, b)], axis=0)

    order = [0, 1] + [d + s for d in near_far for s in (0, 1)] + [d + s for d in rest_far for s in (0, 1)]
    blocks = jnp.stack([here ^ d for d in order])
    key_pos = (key_map[blocks][:, None] * key_rows + jnp.arange(key_rows, dtype=jnp.int32)[None, :]).reshape(1, -1)
    if order != sorted(order):
        index_keys = jnp.concatenate([index_keys[d * key_rows : (d + 1) * key_rows] for d in order], axis=0)
    places = jnp.stack([offsets[0], rank]).astype(jnp.int32)
    own_pos = (offsets[0] + rank * own_rows).reshape(1).astype(jnp.int32)

    def head_sums(first, key_list):
        size = sum(k.shape[0] for k in key_list)
        first = first * key_rows
        sums = mass(places, queries, key_pos[:, first : first + size], key_list, width, ranks)
        return [sums[0]] + [turn(sums[k], k) for k in range(1, ranks)]

    queries = prep(main_q, log_norms, width)
    sums_0 = head_sums(0, [main_k, sibling])

    for d in rest_far:
        for part in (0, 1):
            last = (d & -d) if part == 0 else 1 << (d.bit_length() - 1)
            pieces[d, part] = swap(pieces[d ^ last, part], last)

    def group_of(numbers):
        chosen = []
        for d in numbers:
            own = [pieces[d, 0], pieces[d, 1]]
            chosen += own + [swap(p, 1) for p in own]
        return chosen

    q_flat = index_q.reshape(own_rows * heads, index_width)
    sig, dev, prob = first_pass(own_pos, q_flat, index_keys, index_w, key_pos)
    sums_1 = head_sums(2, group_of(near_far))
    sums_2 = head_sums(2 + 2 * len(near_far), group_of(rest_far))
    grad_q, grad_w, key_terms = second_pass(
        sig, dev, prob, [sums_0, sums_1, sums_2], row_weight[:, None], index_keys, q_flat.T, heads
    )

    blocks_of = {d: key_terms[:, i * key_rows : (i + 1) * key_rows] for i, d in enumerate(order)}
    for bit in [1] + far_bits:
        kept = [d for d in sorted(blocks_of) if not d & bit]
        sent = swap(jnp.stack([blocks_of[d ^ bit] for d in kept]), bit)
        blocks_of = {d: blocks_of[d] + sent[i] for i, d in enumerate(kept)}
    terms = blocks_of[0].T.reshape(ranks, key_rows // ranks, index_width)
    grad_k = lax.dynamic_index_in_dim(terms, rank, 0, keepdims=False)
    for k in range(1, ranks):
        grad_k = grad_k + turn(lax.dynamic_index_in_dim(terms, (rank + k) % ranks, 0, keepdims=False), k)
    return (grad_q.reshape(index_q.shape), grad_w, grad_k)


def solution(mesh):
    placed = (
        P("ctx", "tp"),
        P("ctx", "tp"),
        P("ctx", "tp"),
        P(("ctx", "tp"), None, None),
        P(("ctx", "tp"), None),
        P("ctx", None),
        P(("ctx", "tp")),
        P("ctx"),
        P(),
    )
    return jax.shard_map(
        per_device,
        mesh=mesh,
        in_specs=placed,
        out_specs=(P(("ctx", "tp"), None, None), P(("ctx", "tp"), None), P(("ctx", "tp"), None)),
        check_vma=False,
    )
```

```python
import functools
import math

import jax
import jax.numpy as jnp
from jax import lax
from jax.experimental import pallas as pl
from jax.experimental.pallas import tpu as pltpu
from jax.sharding import PartitionSpec as P

LOG2E = math.log2(math.e)
LN2 = math.log(2.0)
TOP = 120.0
VMEM_BYTES = 56 * 1024 * 1024
BF = jnp.bfloat16
F32 = jnp.float32


SHORT = pl.CostEstimate(flops=0, transcendentals=0, bytes_accessed=1024)


def prep_kernel(width, step_heads, root, q_ref, ln_ref, out_ref):
    heads, rows = ln_ref.shape
    pad, lanes = 256, 128
    cols = step_heads * lanes
    scaled = -root * ln_ref[...]
    high = scaled.astype(BF).astype(F32)
    mid = (scaled - high).astype(BF).astype(F32)
    low = (scaled - high - mid).astype(BF).astype(F32)
    terms = jnp.concatenate([high, mid, low], axis=0).astype(BF)
    column = lax.broadcasted_iota(jnp.int32, (3 * heads, cols), 1)
    source = lax.broadcasted_iota(jnp.int32, (3 * heads, cols), 0)
    head = source % heads - pl.program_id(0) * step_heads
    spare = jnp.where(head % 2 == 0, width - lanes, 0) + source // heads
    place = jnp.where(column == head * lanes + spare, 1.0, 0.0).astype(BF)
    extra = lax.dot_general(
        terms, place, (((0,), (0,)), ((), ())), preferred_element_type=F32
    ).astype(BF)
    lane = lax.broadcasted_iota(jnp.int32, (rows, lanes), 1)
    for h in range(step_heads):
        odd = h % 2
        first = (h // 2) * 2 * width + odd * (2 * width - pad)
        at = h * pad
        kept = lane >= pad - width if odd else lane < width - lanes
        mixed, plain = (0, lanes) if odd else (lanes, 0)
        out_ref[:, at + plain : at + plain + lanes] = q_ref[:, first + plain : first + plain + lanes]
        out_ref[:, at + mixed : at + mixed + lanes] = jnp.where(
            kept, q_ref[:, first + mixed : first + mixed + lanes], extra[:, h * lanes : (h + 1) * lanes]
        )


def prep(main_q, norms_turned, width, step_heads=8):
    rows = main_q.shape[0]
    heads = norms_turned.shape[0]
    return pl.pallas_call(
        functools.partial(prep_kernel, width, step_heads, math.sqrt(width)),
        grid=(heads // step_heads,),
        in_specs=[
            pl.BlockSpec((rows, step_heads * width), lambda i: (0, i)),
            pl.BlockSpec((heads, rows), lambda i: (0, 0)),
        ],
        out_specs=pl.BlockSpec((rows, step_heads * 256), lambda i: (0, i)),
        out_shape=jax.ShapeDtypeStruct((rows, heads * 256), BF),
        compiler_params=pltpu.CompilerParams(vmem_limit_bytes=VMEM_BYTES),
        cost_estimate=SHORT,
        name="prep",
    )(main_q, norms_turned)


def mass_kernel(width, step_heads, n_keys, ranks, pos_ref, kpos_ref, qa_hbm, *refs):
    key_hbm, out_refs = refs[:n_keys], refs[n_keys : n_keys + ranks]
    qa_ref, keys_ref, total_ref, q_sems, k_sems = refs[n_keys + ranks :]
    pad = 256
    factor = LOG2E / math.sqrt(width)
    rows, total = total_ref.shape
    steps = qa_ref.shape[1] // (step_heads * pad)
    copies = []
    for i in range(steps):
        cols = pl.ds(i * step_heads * pad, step_heads * pad)
        group = [pltpu.make_async_copy(qa_hbm.at[:, cols], qa_ref.at[:, cols], q_sems.at[i])]
        cols = pl.ds(i * step_heads * width, step_heads * width)
        first = 0
        for n, k in enumerate(key_hbm):
            at = pl.ds(first, k.shape[0])
            group.append(pltpu.make_async_copy(k.at[:, cols], keys_ref.at[at, cols], k_sems.at[i, n]))
            first += k.shape[0]
        for copy in group:
            copy.start()
        copies.append(group)
    lane = lax.broadcasted_iota(jnp.int32, (total, pad), 1)
    ones_even = jnp.where((lane >= width) & (lane < width + 3), 1.0, 0.0).astype(BF)
    ones_odd = jnp.where(lane < 3, 1.0, 0.0).astype(BF)
    keep_even = jnp.where(lane < width, 1.0, 0.0).astype(BF)
    keep_odd = jnp.where(lane >= pad - width, 1.0, 0.0).astype(BF)

    def one(h):
        first = (h // 2) * 2 * width + (h % 2) * (2 * width - pad)
        keys = keys_ref[:, first : first + pad]
        keys = keys * keep_odd + ones_odd if h % 2 else keys * keep_even + ones_even
        scores = lax.dot_general(
            qa_ref[:, h * pad : (h + 1) * pad], keys, (((1,), (1,)), ((), ())), preferred_element_type=F32
        )
        return jnp.exp2(scores * factor)

    for i in range(steps):
        for copy in copies[i]:
            copy.wait()
        for h in range(i * step_heads, (i + 1) * step_heads, 2):
            both = one(h) + one(h + 1)
            total_ref[...] = both if h == 0 else total_ref[...] + both

    own = rows // ranks
    for k in range(ranks):
        first = lax.rem(pos_ref[1] + k, ranks) * own
        row = pos_ref[0] + first + lax.broadcasted_iota(jnp.int32, out_refs[k].shape, 0)
        mine = total_ref[pl.ds(pl.multiple_of(first, 8), own), :]
        out_refs[k][...] = jnp.where(kpos_ref[...] <= row, mine, 0.0)


def mass(places, qa, kpos, key_list, width, ranks, step_heads=8):
    rows = qa.shape[0]
    heads = qa.shape[1] // 256
    total = sum(k.shape[0] for k in key_list)
    own = rows // ranks
    steps = heads // step_heads
    vmem = pl.BlockSpec(memory_space=pltpu.VMEM)
    return pl.pallas_call(
        functools.partial(mass_kernel, width, step_heads, len(key_list), ranks),
        in_specs=[pl.BlockSpec(memory_space=pltpu.SMEM), vmem]
        + [pl.BlockSpec(memory_space=pl.ANY)] * (1 + len(key_list)),
        out_specs=[vmem] * ranks,
        out_shape=[jax.ShapeDtypeStruct((own, total), F32)] * ranks,
        scratch_shapes=[
            pltpu.VMEM(qa.shape, BF),
            pltpu.VMEM((total, heads * width), BF),
            pltpu.VMEM((rows, total), F32),
            pltpu.SemaphoreType.DMA((steps,)),
            pltpu.SemaphoreType.DMA((steps, len(key_list))),
        ],
        compiler_params=pltpu.CompilerParams(vmem_limit_bytes=VMEM_BYTES),
        cost_estimate=SHORT,
        name="mass",
    )(places, kpos, qa, *key_list)


def in_pairs(steps, load, work, finish):
    pairs = (steps - 1) // 2
    load(0, 0)

    def two(p, _):
        first = 2 * p
        finish(first, 2)
        load(first + 1, 1)
        work(first, 0)
        load(first + 2, 0)
        work(first + 1, 1)
        return 0

    lax.fori_loop(0, pairs, two, 0)
    last = 2 * pairs
    if steps % 2 == 0:
        finish(last, 2)
        load(last + 1, 1)
        work(last, 0)
        work(last + 1, 1)
    else:
        finish(last, 1)
        work(last, 0)


def tile_of(i, size):
    return pl.ds(i * size if isinstance(i, int) else pl.multiple_of(i * size, size), size)


def first_kernel(rows, scale, pos_ref, q_ref, key_ref, w_ref, kpos_ref, power_hbm, prob_ref, raw_0, raw_1, ring, sems):
    keys = key_ref.shape[0]
    own, heads = w_ref.shape
    span = rows * heads
    steps = own // rows
    raws = (raw_0, raw_1)
    slots = ring.shape[0]

    def copy_out(i):
        slot = i % slots if isinstance(i, int) else lax.rem(i, slots)
        return pltpu.make_async_copy(ring.at[slot], power_hbm.at[tile_of(i, span), :], sems.at[slot])

    def multiply(i, slot):
        raws[slot][...] = lax.dot_general(
            q_ref[tile_of(i, span), :], key_ref[...], (((1,), (1,)), ((), ())), preferred_element_type=F32
        )

    def finish(i, count):
        for n in range(count):
            if isinstance(i, int):
                if i + n >= slots:
                    copy_out(i + n - slots).wait()
            else:

                @pl.when(i + n >= slots)
                def _():
                    copy_out(i + n - slots).wait()

    def elements(i, slot):
        raw = raws[slot]
        where = i % slots if isinstance(i, int) else lax.rem(i, slots)
        w_turned = jnp.transpose(w_ref[tile_of(i, rows), :]) * LN2
        logits = []
        for t in range(rows):
            w = w_turned[:, t : t + 1]
            parts = []
            for c in range(keys // 128):
                at = (slice(t * heads, (t + 1) * heads), slice(c * 128, (c + 1) * 128))
                u = raw[at] * (scale * LOG2E)
                power = jnp.exp2(jnp.minimum(u, TOP))
                ring[(where, *at)] = power
                soft = jnp.maximum(u, jnp.log2(1.0 + power))
                parts.append(jnp.sum(w * soft, axis=0, keepdims=True))
            logits.append(jnp.concatenate(parts, axis=1))
        prob_ref[tile_of(i, rows), :] = jnp.concatenate(logits, axis=0)
        copy_out(i).start()

    in_pairs(steps, multiply, elements, finish)
    row = pos_ref[0] + lax.broadcasted_iota(jnp.int32, prob_ref.shape, 0)
    masked = jnp.where(kpos_ref[...] <= row, prob_ref[...], -jnp.inf)
    top = jnp.max(masked, axis=1, keepdims=True)
    terms = jnp.exp2((masked - top) * LOG2E)
    prob_ref[...] = terms / jnp.sum(terms, axis=1, keepdims=True)
    for i in range(max(steps - slots, 0), steps):
        copy_out(i).wait()


def first_pass(own_pos, q_flat, keys, weights, kpos, rows=8, slots=4):
    total, width = q_flat.shape
    key_total = keys.shape[0]
    own, heads = weights.shape
    tile = rows * heads
    vmem = pl.BlockSpec(memory_space=pltpu.VMEM)
    return pl.pallas_call(
        functools.partial(first_kernel, rows, 1.0 / math.sqrt(width)),
        in_specs=[pl.BlockSpec(memory_space=pltpu.SMEM), vmem, vmem, vmem, vmem],
        out_specs=[pl.BlockSpec(memory_space=pl.ANY), vmem],
        out_shape=[
            jax.ShapeDtypeStruct((total, key_total), F32),
            jax.ShapeDtypeStruct((own, key_total), F32),
        ],
        scratch_shapes=[
            pltpu.VMEM((tile, key_total), F32),
            pltpu.VMEM((tile, key_total), F32),
            pltpu.VMEM((slots, tile, key_total), F32),
            pltpu.SemaphoreType.DMA((slots,)),
        ],
        compiler_params=pltpu.CompilerParams(vmem_limit_bytes=VMEM_BYTES),
        cost_estimate=SHORT,
        name="first_pass",
    )(own_pos, q_flat, keys, weights, kpos)


def second_kernel(rows, splits, cuts, columns, scale, big_ref, rw_ref, w_ref, key_ref, qt_ref, *refs):
    powers, probs, refs = refs[:cuts], refs[cuts : 2 * cuts], refs[2 * cuts :]
    count = sum(splits)
    parts, refs = refs[:count], refs[count:]
    gq_hbm, gw_ref, mine_ref, theirs_ref, power_ref, out_ref, coef_ref, grad_0, grad_1, sems, out_sems = refs
    grads = (grad_0, grad_1)
    keys = key_ref.shape[0]
    own, heads = w_ref.shape
    tile = rows * heads
    steps = own // rows
    lane = lax.broadcasted_iota(jnp.int32, (heads, 128), 1)

    def copy_in(i, source=powers[0], first=0):
        return pltpu.make_async_copy(source.at[tile_of(first, tile), :], power_ref.at[tile_of(i, tile), :], sems.at[i])

    def copy_out(i):
        at = tile_of(i, tile)
        return pltpu.make_async_copy(out_ref.at[at, :], gq_hbm.at[at, :], out_sems.at[i])

    done = 0
    for source in powers:
        count = source.shape[0] // tile
        for i in range(count):
            copy_in(done + i, source, i).start()
        done += count
    groups = []
    for size in splits:
        groups.append(sum(r[...] for r in parts[:size]))
        parts = parts[size:]
    span = keys // len(columns)
    mass_rows = jnp.concatenate([groups[g][:, n * span : (n + 1) * span] for g, n in columns], axis=1)
    target = mass_rows / jnp.sum(mass_rows, axis=1, keepdims=True)
    coef_ref[...] = rw_ref[...] * (jnp.concatenate([r[...] for r in probs], axis=0) - target)
    mine_ref[...] = jnp.zeros_like(mine_ref)
    theirs_ref[...] = jnp.zeros_like(theirs_ref)
    side = keys // 2

    def lanes_of(columns):
        block = jnp.zeros((heads, 128), F32)
        for t, column in enumerate(columns):
            block = jnp.where(lane == t, column, block)
        return jnp.transpose(block)[:rows, :]

    def elements(i, slot):
        coef = coef_ref[tile_of(i, rows), :]
        w_turned = jnp.transpose(w_ref[tile_of(i, rows), :]) * scale
        columns = []
        for t in range(rows):
            w = w_turned[:, t : t + 1]
            total = jnp.zeros((heads, 128), F32)
            from_row = tile_of(i * rows + t, heads)
            for c in range(keys // 128):
                cols = slice(c * 128, (c + 1) * 128)
                row = coef[t : t + 1, cols]
                power = power_ref[from_row, cols]
                up = 1.0 + power
                grads[slot][t * heads : (t + 1) * heads, cols] = (
                    power * pl.reciprocal(up, approx=False) * (row * w)
                ).astype(BF)
                total = total + jnp.log2(up) * row
            columns.append(jnp.sum(total, axis=1, keepdims=True))
        gw_ref[tile_of(i, rows), :] = lanes_of(columns) * LN2

    def multiply(i, slot):
        block = grads[slot][...]
        at = tile_of(i, tile)
        out_ref[at, :] = jnp.dot(block, key_ref[...], preferred_element_type=F32)
        mine_ref[...] += jnp.dot(qt_ref[:, at], block[:, :side], preferred_element_type=F32)
        theirs_ref[...] += jnp.dot(qt_ref[:, at], block[:, side:], preferred_element_type=F32)

    def finish(i, number):
        for n in range(1, number + 1):
            if isinstance(i, int):
                if i + n < steps:
                    copy_in(i + n).wait()
            else:
                copy_in(i + n).wait()

    copy_in(0).wait()
    in_pairs(steps, elements, multiply, finish)
    for i in range(steps):
        copy_out(i).start()

    @pl.when(big_ref[0] > 0)
    def _():
        def past_top(i, _):
            raw = lax.dot_general(
                qt_ref[:, tile_of(i, tile)], key_ref[...], (((0,), (1,)), ((), ())), preferred_element_type=F32
            )
            over = jnp.maximum(raw * (scale * LOG2E) - TOP, 0.0)
            coef = coef_ref[tile_of(i, rows), :]
            columns = [
                jnp.sum(over[t * heads : (t + 1) * heads, :] * coef[t : t + 1, :], axis=1, keepdims=True)
                for t in range(rows)
            ]
            gw_ref[tile_of(i, rows), :] += lanes_of(columns) * LN2
            return 0

        lax.fori_loop(0, steps, past_top, 0)

    for i in range(steps):
        copy_out(i).wait()


def may_pass_top(q_flat, keys):
    q_most = jnp.max(jnp.sum(jnp.square(q_flat.astype(F32)), axis=1))
    k_most = jnp.max(jnp.sum(jnp.square(keys.astype(F32)), axis=1))
    bound = q_most * k_most * (LOG2E * LOG2E / q_flat.shape[1])
    return (bound > (TOP - 1.0) ** 2).astype(jnp.int32).reshape(1)


def second_pass(big, powers, probs, mass_parts, columns, row_weight, weights, keys, q_turned, rows=8):
    key_total = keys.shape[0]
    total = q_turned.shape[1]
    own, heads = weights.shape
    tile = rows * heads
    steps = own // rows
    width = keys.shape[1]
    flat = [piece for pieces in mass_parts for piece in pieces]
    vmem = pl.BlockSpec(memory_space=pltpu.VMEM)
    hbm = pl.BlockSpec(memory_space=pl.ANY)
    return pl.pallas_call(
        functools.partial(
            second_kernel,
            rows,
            tuple(len(p) for p in mass_parts),
            len(powers),
            columns,
            1.0 / math.sqrt(width),
        ),
        in_specs=[pl.BlockSpec(memory_space=pltpu.SMEM)]
        + [vmem] * 4
        + [hbm] * len(powers)
        + [vmem] * (len(probs) + len(flat)),
        out_specs=[hbm, vmem, vmem, vmem],
        out_shape=[
            jax.ShapeDtypeStruct((total, width), F32),
            jax.ShapeDtypeStruct((own, heads), F32),
            jax.ShapeDtypeStruct((width, key_total // 2), F32),
            jax.ShapeDtypeStruct((width, key_total // 2), F32),
        ],
        scratch_shapes=[
            pltpu.VMEM((total, key_total), F32),
            pltpu.VMEM((total, width), F32),
            pltpu.VMEM((own, key_total), F32),
            pltpu.VMEM((tile, key_total), BF),
            pltpu.VMEM((tile, key_total), BF),
            pltpu.SemaphoreType.DMA((steps,)),
            pltpu.SemaphoreType.DMA((steps,)),
        ],
        compiler_params=pltpu.CompilerParams(vmem_limit_bytes=VMEM_BYTES),
        cost_estimate=SHORT,
        name="second_pass",
    )(big, row_weight, weights, keys, q_turned, *powers, *probs, *flat)


def swap(x, bit):
    size = lax.axis_size("ctx")
    return lax.ppermute(x, "ctx", [(i, i ^ bit) for i in range(size)])


def turn(x, steps):
    size = lax.axis_size("tp")
    return lax.ppermute(x, "tp", [(i, (i + steps) % size) for i in range(size)])


def together(*values):
    return lax.optimization_barrier(values)


def after(x, *others):
    return lax.optimization_barrier((x, *others))[0]


def per_device(main_q, main_k, log_norms, index_q, index_w, index_k, row_weight, offsets, key_map):
    key_rows = main_k.shape[0]
    own_rows, heads, index_width = index_q.shape
    main_heads = log_norms.shape[1]
    width = main_k.shape[1] // main_heads
    places_ctx = lax.axis_size("ctx")
    ranks = lax.axis_size("tp")
    here = lax.axis_index("ctx")
    rank = lax.axis_index("tp")
    far_bits = [b for b in (2**i for i in range(1, places_ctx.bit_length() - 1))]
    sums_of_bits = [sum(b for i, b in enumerate(far_bits) if n >> i & 1) for n in range(1, 2 ** len(far_bits))]
    near_far = [d for d in sums_of_bits if d & (d - 1) == 0]
    rest_far = sorted((d for d in sums_of_bits if d & (d - 1) != 0), key=int.bit_count)

    queries = prep(main_q, log_norms.T, width)
    index_far = [swap(index_k, d) for d in near_far + rest_far]
    main_k, index_k, *index_far = together(main_k, index_k, *index_far)
    keys_at = {0: main_k}
    for d in near_far:
        keys_at[d] = swap(main_k, d)
    keys_at[1] = swap(main_k, 1)
    index_w, row_weight, offsets, key_map, index_q, index_k, queries = together(
        index_w, row_weight, offsets, key_map, index_q, index_k, queries
    )
    index_mine = [index_k] + index_far
    index_theirs = swap(jnp.stack(index_mine), 1)
    far = [0] + near_far + rest_far
    order = far + [d + 1 for d in far]
    blocks = jnp.stack([here ^ d for d in order])
    key_pos = key_map[blocks][:, None] * key_rows + jnp.arange(key_rows, dtype=jnp.int32)[None, :]
    index_keys = jnp.concatenate([*index_mine, index_theirs.reshape(-1, index_width)], axis=0)
    own_pos = (offsets[0] + rank * own_rows).reshape(1).astype(jnp.int32)

    def head_sums(members, parts):
        places = jnp.stack([offsets[0], rank if parts > 1 else 0 * rank]).astype(jnp.int32)
        group_pos = jnp.concatenate([key_pos[order.index(d)] for d in members]).reshape(1, -1)
        return mass(places, queries, group_pos, [keys_at[d] for d in members], width, parts)

    def to_owners(sums):
        return [sums[0]] + [turn(sums[k], k) for k in range(1, ranks)]

    q_flat = index_q.reshape(own_rows * heads, index_width)
    q_turned = q_flat.T
    big = may_pass_top(q_flat, index_keys)
    row_weight = row_weight[:, None]
    tiles = own_rows // 8
    ends = [0, tiles * 5 // 7, tiles]
    powers, probs = [], []

    def index_part(n, *others):
        first, last = ends[n] * 8, ends[n + 1] * 8
        rows = after(q_flat[first * heads : last * heads], *others)
        power, prob = first_pass(own_pos + first, rows, index_keys, index_w[first:last], key_pos.reshape(1, -1))
        powers.append(power)
        probs.append(prob)
        return prob

    group_own = [0, 1]
    group_near = [d + side for d in near_far for side in (0, 1)]
    group_rest = [d + side for d in rest_far for side in (0, 1)]
    groups = [group_own, group_near, group_rest]
    columns = tuple((n, group.index(d)) for d in order for n, group in enumerate(groups) if d in group)

    sums_own = head_sums(group_own, 1)[0]
    part_0 = index_part(0, sums_own)
    sums_own = lax.psum_scatter(sums_own, "tp", scatter_dimension=0, tiled=True)
    part_0, sums_own, *got = together(part_0, sums_own, *[keys_at[d] for d in near_far])
    keys_at.update(zip(near_far, got))
    for d in rest_far:
        lowest, highest = d & -d, 1 << (d.bit_length() - 1)
        source = jnp.where(here % 2 == 0, keys_at[d ^ lowest], keys_at[d ^ highest])
        keys_at[d] = lax.ppermute(
            source, "ctx", [(i, i ^ (highest if i % 2 else lowest)) for i in range(places_ctx)]
        )
    for d in near_far:
        keys_at[d + 1] = swap(keys_at[d], 1)
    sums_near = head_sums(group_near, ranks)
    got = together(sums_near[0], *[keys_at[d] for d in rest_far])
    keys_at.update(zip(rest_far, got[1:]))
    for d in rest_far:
        keys_at[d + 1] = swap(keys_at[d], 1)
    sums_near = to_owners(sums_near)
    sums_rest = head_sums(group_rest, ranks)
    index_part(1, sums_rest[0])
    sums_rest = to_owners(sums_rest)
    grad_q, grad_w, mine, theirs = second_pass(
        big, powers, probs, [[sums_own], sums_near, sums_rest], columns, row_weight, index_w, index_keys, q_turned
    )

    mine = mine + swap(theirs, 1)
    terms = mine[:, :key_rows]
    for n, d in enumerate(far[1:], 1):
        terms = terms + swap(mine[:, n * key_rows : (n + 1) * key_rows], d)
    terms = terms.T.reshape(ranks, key_rows // ranks, index_width)
    grad_k = lax.dynamic_index_in_dim(terms, rank, 0, keepdims=False)
    for k in range(1, ranks):
        grad_k = grad_k + turn(lax.dynamic_index_in_dim(terms, (rank + k) % ranks, 0, keepdims=False), k)
    return (grad_q.reshape(index_q.shape), grad_w, grad_k)


def solution(mesh):
    placed = (
        P("ctx", "tp"),
        P("ctx", "tp"),
        P("ctx", "tp"),
        P(("ctx", "tp"), None, None),
        P(("ctx", "tp"), None),
        P("ctx", None),
        P(("ctx", "tp")),
        P("ctx"),
        P(),
    )
    return jax.shard_map(
        per_device,
        mesh=mesh,
        in_specs=placed,
        out_specs=(P(("ctx", "tp"), None, None), P(("ctx", "tp"), None), P(("ctx", "tp"), None)),
        check_vma=False,
    )
```

```python
import functools
import math

import jax
import jax.numpy as jnp
from jax import lax
from jax.experimental import pallas as pl
from jax.experimental.pallas import tpu as pltpu
from jax.sharding import PartitionSpec as P

LOG2E = math.log2(math.e)
LN2 = math.log(2.0)
TOP = 120.0
VMEM_BYTES = 56 * 1024 * 1024
BF = jnp.bfloat16
F32 = jnp.float32


SHORT = pl.CostEstimate(flops=0, transcendentals=0, bytes_accessed=1024)


def prep_kernel(width, step_heads, root, q_ref, ln_ref, out_ref):
    heads, rows = ln_ref.shape
    pad, lanes = 256, 128
    cols = step_heads * lanes
    scaled = -root * ln_ref[...]
    high = scaled.astype(BF).astype(F32)
    mid = (scaled - high).astype(BF).astype(F32)
    low = (scaled - high - mid).astype(BF).astype(F32)
    terms = jnp.concatenate([high, mid, low], axis=0).astype(BF)
    column = lax.broadcasted_iota(jnp.int32, (3 * heads, cols), 1)
    source = lax.broadcasted_iota(jnp.int32, (3 * heads, cols), 0)
    head = source % heads - pl.program_id(0) * step_heads
    spare = jnp.where(head % 2 == 0, width - lanes, 0) + source // heads
    place = jnp.where(column == head * lanes + spare, 1.0, 0.0).astype(BF)
    extra = lax.dot_general(
        terms, place, (((0,), (0,)), ((), ())), preferred_element_type=F32
    ).astype(BF)
    lane = lax.broadcasted_iota(jnp.int32, (rows, lanes), 1)
    for h in range(step_heads):
        odd = h % 2
        first = (h // 2) * 2 * width + odd * (2 * width - pad)
        at = h * pad
        kept = lane >= pad - width if odd else lane < width - lanes
        mixed, plain = (0, lanes) if odd else (lanes, 0)
        out_ref[:, at + plain : at + plain + lanes] = q_ref[:, first + plain : first + plain + lanes]
        out_ref[:, at + mixed : at + mixed + lanes] = jnp.where(
            kept, q_ref[:, first + mixed : first + mixed + lanes], extra[:, h * lanes : (h + 1) * lanes]
        )


def prep(main_q, norms_turned, width, step_heads=8):
    rows = main_q.shape[0]
    heads = norms_turned.shape[0]
    return pl.pallas_call(
        functools.partial(prep_kernel, width, step_heads, math.sqrt(width)),
        grid=(heads // step_heads,),
        in_specs=[
            pl.BlockSpec((rows, step_heads * width), lambda i: (0, i)),
            pl.BlockSpec((heads, rows), lambda i: (0, 0)),
        ],
        out_specs=pl.BlockSpec((rows, step_heads * 256), lambda i: (0, i)),
        out_shape=jax.ShapeDtypeStruct((rows, heads * 256), BF),
        compiler_params=pltpu.CompilerParams(vmem_limit_bytes=VMEM_BYTES),
        cost_estimate=SHORT,
        name="prep",
    )(main_q, norms_turned)


def mass_kernel(width, step_heads, members, ranks, whole, pos_ref, qa_hbm, *refs):
    n_keys = len(members)
    key_hbm, out_refs = refs[:n_keys], refs[n_keys : n_keys + ranks]
    qa_ref, keys_ref, total_ref, q_sems, k_sems = refs[n_keys + ranks :]
    pad = 256
    factor = LOG2E / math.sqrt(width)
    rows, total = total_ref.shape
    steps = qa_ref.shape[1] // (step_heads * pad)
    copies = []
    for i in range(steps):
        cols = pl.ds(i * step_heads * pad, step_heads * pad)
        group = [pltpu.make_async_copy(qa_hbm.at[:, cols], qa_ref.at[:, cols], q_sems.at[i])]
        cols = pl.ds(i * step_heads * width, step_heads * width)
        first = 0
        for n, k in enumerate(key_hbm):
            at = pl.ds(first, k.shape[0])
            group.append(pltpu.make_async_copy(k.at[:, cols], keys_ref.at[at, cols], k_sems.at[i, n]))
            first += k.shape[0]
        copies.append(group)
    for group in copies[:2]:
        for copy in group:
            copy.start()
    lane = lax.broadcasted_iota(jnp.int32, (total, pad), 1)
    ones_even = jnp.where((lane >= width) & (lane < width + 3), 1.0, 0.0).astype(BF)
    ones_odd = jnp.where(lane < 3, 1.0, 0.0).astype(BF)
    keep_even = jnp.where(lane < width, 1.0, 0.0).astype(BF)
    keep_odd = jnp.where(lane >= pad - width, 1.0, 0.0).astype(BF)

    def one(h):
        first = (h // 2) * 2 * width + (h % 2) * (2 * width - pad)
        keys = keys_ref[:, first : first + pad]
        keys = keys * keep_odd + ones_odd if h % 2 else keys * keep_even + ones_even
        scores = lax.dot_general(
            qa_ref[:, h * pad : (h + 1) * pad], keys, (((1,), (1,)), ((), ())), preferred_element_type=F32
        )
        return jnp.exp2(scores * factor)

    for i in range(steps):
        for copy in copies[i]:
            copy.wait()
        for copy in copies[i + 2] if i + 2 < steps else []:
            copy.start()
        for h in range(i * step_heads, (i + 1) * step_heads, 2):
            both = one(h) + one(h + 1)
            total_ref[...] = both if h == 0 else total_ref[...] + both

    own = rows // ranks
    for k in range(ranks):
        first = 0 if whole else lax.rem(pos_ref[1] + k, ranks) * own
        column = 0
        for place, keys in zip(members, key_hbm):
            size = keys.shape[0]
            shape = (own, size)
            row = pos_ref[0] + first + lax.broadcasted_iota(jnp.int32, shape, 0)
            key = pos_ref[2 + place[0]] + place[1] + lax.broadcasted_iota(jnp.int32, shape, 1)
            mine = total_ref[tile_of(first, 1, own), column : column + size]
            out_refs[k][:, column : column + size] = jnp.where(key <= row, mine, 0.0)
            column += size


def mass(places, qa, members, key_list, width, ranks, step_heads=8):
    rows = qa.shape[0]
    heads = qa.shape[1] // 256
    total = sum(k.shape[0] for k in key_list)
    whole = ranks == 1
    hbm = pl.BlockSpec(memory_space=pltpu.HBM)
    own = rows // ranks
    steps = heads // step_heads
    vmem = pl.BlockSpec(memory_space=pltpu.VMEM)
    return pl.pallas_call(
        functools.partial(mass_kernel, width, step_heads, tuple(members), ranks, whole),
        in_specs=[pl.BlockSpec(memory_space=pltpu.SMEM), hbm] + [hbm] * len(key_list),
        out_specs=[vmem] * ranks,
        out_shape=[jax.ShapeDtypeStruct((own, total), F32)] * ranks,
        scratch_shapes=[
            pltpu.VMEM(qa.shape, BF),
            pltpu.VMEM((total, heads * width), BF),
            pltpu.VMEM((rows, total), F32),
            pltpu.SemaphoreType.DMA((steps,)),
            pltpu.SemaphoreType.DMA((steps, len(key_list))),
        ],
        compiler_params=pltpu.CompilerParams(vmem_limit_bytes=VMEM_BYTES),
        cost_estimate=SHORT,
        name="mass",
    )(places, qa, *key_list)


def in_pairs(steps, load, work, finish):
    pairs = (steps - 1) // 2
    load(0, 0)

    def two(p, _):
        first = 2 * p
        finish(first, 2)
        load(first + 1, 1)
        work(first, 0)
        load(first + 2, 0)
        work(first + 1, 1)
        return 0

    lax.fori_loop(0, pairs, two, 0)
    last = 2 * pairs
    if steps % 2 == 0:
        finish(last, 2)
        load(last + 1, 1)
        work(last, 0)
        work(last + 1, 1)
    else:
        finish(last, 1)
        work(last, 0)


def tile_of(i, step, size=None):
    size = step if size is None else size
    return pl.ds(i * step if isinstance(i, int) else pl.multiple_of(i * step, max(step, 8)), size)


def first_kernel(rows, scale, start, pos_ref, q_ref, key_ref, w_ref, power_hbm, prob_ref, most_ref, raw_0, raw_1, logits, ring, sems):
    keys = key_ref.shape[0]
    own, heads = w_ref.shape
    span = rows * heads
    steps = own // rows
    raws = (raw_0, raw_1)
    slots = ring.shape[0]

    def copy_out(i):
        slot = i % slots if isinstance(i, int) else lax.rem(i, slots)
        return pltpu.make_async_copy(ring.at[slot], power_hbm.at[tile_of(i, span), :], sems.at[slot])

    def multiply(i, slot):
        raws[slot][...] = lax.dot_general(
            q_ref[tile_of(i, span), :], key_ref[...], (((1,), (1,)), ((), ())), preferred_element_type=F32
        )

    def finish(i, count):
        for n in range(count):
            if isinstance(i, int):
                if i + n >= slots:
                    copy_out(i + n - slots).wait()
            else:

                @pl.when(i + n >= slots)
                def _():
                    copy_out(i + n - slots).wait()

    def elements(capped, i, slot):
        raw = raws[slot]
        where = i % slots if isinstance(i, int) else lax.rem(i, slots)
        w_turned = jnp.transpose(w_ref[tile_of(i, rows), :]) * LN2
        for t in range(rows):
            w = w_turned[:, t : t + 1]
            for c in range(keys // 128):
                at = (slice(t * heads, (t + 1) * heads), slice(c * 128, (c + 1) * 128))
                u = raw[at] * (scale * LOG2E)
                power = jnp.exp2(jnp.minimum(u, TOP) if capped else u)
                ring[(where, *at)] = power
                soft = jnp.log2(1.0 + power)
                soft = jnp.maximum(u, soft) if capped else soft
                logits[slot, t : t + 1, c * 128 : (c + 1) * 128] = jnp.sum(w * soft, axis=0, keepdims=True)
        prob_ref[tile_of(i, rows), :] = logits[slot]
        copy_out(i).start()

    q_most = jnp.zeros((8, 1), F32)
    for i in range(steps):
        part = jnp.sum(jnp.square(q_ref[tile_of(i, span), :].astype(F32)), axis=1, keepdims=True)
        q_most = jnp.maximum(q_most, jnp.max(part.reshape(-1, 8, 1), axis=0))
    k_most = jnp.max(jnp.sum(jnp.square(key_ref[...].astype(F32)), axis=1, keepdims=True))
    most_ref[...] = jnp.broadcast_to(q_most * (k_most * (scale * LOG2E) ** 2), most_ref.shape)
    past_top = jnp.max(most_ref[...]) > (TOP - 1.0) ** 2

    @pl.when(jnp.logical_not(past_top))
    def _():
        in_pairs(steps, multiply, functools.partial(elements, False), finish)

    @pl.when(past_top)
    def _():
        in_pairs(steps, multiply, functools.partial(elements, True), finish)

    blocks = pos_ref.shape[0] - 2
    size = keys // blocks
    row = pos_ref[0] + pos_ref[1] * start[1] + start[0] + lax.broadcasted_iota(jnp.int32, (own, size), 0)
    lane = lax.broadcasted_iota(jnp.int32, (own, size), 1)
    masked = jnp.concatenate(
        [
            jnp.where(pos_ref[2 + n] + lane <= row, prob_ref[:, n * size : (n + 1) * size], -jnp.inf)
            for n in range(blocks)
        ],
        axis=1,
    )
    top = jnp.max(masked, axis=1, keepdims=True)
    terms = jnp.exp2((masked - top) * LOG2E)
    prob_ref[...] = terms / jnp.sum(terms, axis=1, keepdims=True)
    for i in range(max(steps - slots, 0), steps):
        copy_out(i).wait()


def first_pass(places, start, q_flat, keys, weights, rows=8, slots=4):
    total, width = q_flat.shape
    key_total = keys.shape[0]
    own, heads = weights.shape
    tile = rows * heads
    vmem = pl.BlockSpec(memory_space=pltpu.VMEM)
    return pl.pallas_call(
        functools.partial(first_kernel, rows, 1.0 / math.sqrt(width), start),
        in_specs=[pl.BlockSpec(memory_space=pltpu.SMEM), vmem, vmem, vmem],
        out_specs=[pl.BlockSpec(memory_space=pltpu.HBM), vmem, vmem],
        out_shape=[
            jax.ShapeDtypeStruct((total, key_total), F32),
            jax.ShapeDtypeStruct((own, key_total), F32),
            jax.ShapeDtypeStruct((8, 128), F32),
        ],
        scratch_shapes=[
            pltpu.VMEM((tile, key_total), F32),
            pltpu.VMEM((tile, key_total), F32),
            pltpu.VMEM((2, rows, key_total), F32),
            pltpu.VMEM((slots, tile, key_total), F32),
            pltpu.SemaphoreType.DMA((slots,)),
        ],
        compiler_params=pltpu.CompilerParams(vmem_limit_bytes=VMEM_BYTES),
        cost_estimate=SHORT,
        name="first_pass",
    )(places, q_flat, keys, weights)


def second_kernel(rows, splits, cuts, columns, scale, rw_ref, w_ref, key_ref, q_ref, *refs):
    powers, probs, mosts, refs = refs[:cuts], refs[cuts : 2 * cuts], refs[2 * cuts : 3 * cuts], refs[3 * cuts :]
    count = sum(splits)
    parts, refs = refs[:count], refs[count:]
    gq_hbm, gw_ref, mine_ref, theirs_ref, power_ref, out_ref, coef_ref, grad_0, grad_1, sems, out_sems = refs
    grads = (grad_0, grad_1)
    keys = key_ref.shape[0]
    own, heads = w_ref.shape
    tile = rows * heads
    steps = own // rows
    lane = lax.broadcasted_iota(jnp.int32, (heads, 128), 1)

    def copy_in(i, source=powers[0], first=0):
        return pltpu.make_async_copy(source.at[tile_of(first, tile), :], power_ref.at[tile_of(i, tile), :], sems.at[i])

    def copy_out(i):
        at = tile_of(i, tile)
        return pltpu.make_async_copy(out_ref.at[at, :], gq_hbm.at[at, :], out_sems.at[i])

    sources = [(source, i) for source in powers for i in range(source.shape[0] // tile)]
    runs = [0]
    for source in powers:
        runs.append(runs[-1] + source.shape[0] // tile)

    def start_in(i):
        if isinstance(i, int):
            if i < steps:
                copy_in(i, *sources[i]).start()
        else:
            for source, low, high in zip(powers, runs, runs[1:]):

                @pl.when((i >= low) & (i < high))
                def _():
                    copy_in(i, source, i - low).start()

    for i in range(3):
        start_in(i)
    groups = []
    for size in splits:
        groups.append(sum(r[...] for r in parts[:size]))
        parts = parts[size:]
    span = keys // len(columns)
    mass_rows = jnp.concatenate([groups[g][:, n * span : (n + 1) * span] for g, n in columns], axis=1)
    target = mass_rows / jnp.sum(mass_rows, axis=1, keepdims=True)
    coef_ref[...] = rw_ref[...] * (jnp.concatenate([r[...] for r in probs], axis=0) - target)
    mine_ref[...] = jnp.zeros_like(mine_ref)
    theirs_ref[...] = jnp.zeros_like(theirs_ref)
    side = keys // 2

    def add_column(block, t, values):
        return jnp.where(lane == t, jnp.sum(values, axis=1, keepdims=True), block)

    def as_rows(block):
        return jnp.transpose(block)[:rows, :] * LN2

    def elements(i, slot):
        coef = coef_ref[tile_of(i, rows), :]
        w_turned = jnp.transpose(w_ref[tile_of(i, rows), :]) * scale
        block = jnp.zeros((heads, 128), F32)
        for t in range(rows):
            w = w_turned[:, t : t + 1]
            total = jnp.zeros((heads, 128), F32)
            from_row = tile_of(i * rows + t, heads)
            for c in range(keys // 128):
                cols = slice(c * 128, (c + 1) * 128)
                row = coef[t : t + 1, cols]
                power = power_ref[from_row, cols]
                up = 1.0 + power
                grads[slot][t * heads : (t + 1) * heads, cols] = (
                    power * pl.reciprocal(up, approx=False) * (row * w)
                ).astype(BF)
                total = total + jnp.log2(up) * row
            block = add_column(block, t, total)
        gw_ref[tile_of(i, rows), :] = as_rows(block)

    def multiply(i, slot):
        block = grads[slot][...]
        at = tile_of(i, tile)
        out_ref[at, :] = jnp.dot(block, key_ref[...], preferred_element_type=F32)
        turned = jnp.transpose(q_ref[at, :])
        mine_ref[...] += jnp.dot(turned, block[:, :side], preferred_element_type=F32)
        theirs_ref[...] += jnp.dot(turned, block[:, side:], preferred_element_type=F32)
        copy_out(i).start()

    def finish(i, number):
        for n in range(1, number + 1):
            if not isinstance(i, int) or i + n < steps:
                copy_in(i + n).wait()
        for n in range(1, number + 1):
            start_in(i + number + n)

    copy_in(0).wait()
    in_pairs(steps, elements, multiply, finish)
    most = functools.reduce(jnp.maximum, [r[...] for r in mosts])

    @pl.when(jnp.max(most) > (TOP - 1.0) ** 2)
    def _():
        def past_top(i, _):
            raw = lax.dot_general(
                q_ref[tile_of(i, tile), :], key_ref[...], (((1,), (1,)), ((), ())), preferred_element_type=F32
            )
            over = jnp.maximum(raw * (scale * LOG2E) - TOP, 0.0)
            coef = coef_ref[tile_of(i, rows), :]
            block = jnp.zeros((heads, 128), F32)
            for t in range(rows):
                block = add_column(block, t, over[t * heads : (t + 1) * heads, :] * coef[t : t + 1, :])
            gw_ref[tile_of(i, rows), :] += as_rows(block)
            return 0

        lax.fori_loop(0, steps, past_top, 0)

    for i in range(steps):
        copy_out(i).wait()


def second_pass(firsts, mass_parts, columns, row_weight, weights, keys, q_flat, rows=8):
    powers, probs, mosts = zip(*firsts)
    key_total = keys.shape[0]
    total = q_flat.shape[0]
    own, heads = weights.shape
    tile = rows * heads
    steps = own // rows
    width = keys.shape[1]
    flat = [piece for pieces in mass_parts for piece in pieces]
    vmem = pl.BlockSpec(memory_space=pltpu.VMEM)
    hbm = pl.BlockSpec(memory_space=pltpu.HBM)
    return pl.pallas_call(
        functools.partial(
            second_kernel,
            rows,
            tuple(len(p) for p in mass_parts),
            len(powers),
            columns,
            1.0 / math.sqrt(width),
        ),
        in_specs=[vmem] * 4 + [hbm] * len(powers) + [vmem] * (2 * len(probs) + len(flat)),
        out_specs=[hbm, vmem, vmem, vmem],
        out_shape=[
            jax.ShapeDtypeStruct((total, width), F32),
            jax.ShapeDtypeStruct((own, heads), F32),
            jax.ShapeDtypeStruct((width, key_total // 2), F32),
            jax.ShapeDtypeStruct((width, key_total // 2), F32),
        ],
        scratch_shapes=[
            pltpu.VMEM((total, key_total), F32),
            pltpu.VMEM((total, width), F32),
            pltpu.VMEM((own, key_total), F32),
            pltpu.VMEM((tile, key_total), BF),
            pltpu.VMEM((tile, key_total), BF),
            pltpu.SemaphoreType.DMA((steps,)),
            pltpu.SemaphoreType.DMA((steps,)),
        ],
        compiler_params=pltpu.CompilerParams(vmem_limit_bytes=VMEM_BYTES),
        cost_estimate=SHORT,
        name="second_pass",
    )(row_weight, weights, keys, q_flat, *powers, *probs, *mosts, *flat)


def swap(x, bit):
    size = lax.axis_size("ctx")
    return lax.ppermute(x, "ctx", [(i, i ^ bit) for i in range(size)])


def turn(x, steps):
    size = lax.axis_size("tp")
    return lax.ppermute(x, "tp", [(i, (i + steps) % size) for i in range(size)])


def together(*values):
    return lax.optimization_barrier(values)


def after(x, *others):
    return lax.optimization_barrier((x, *others))[0]


def per_device(main_q, main_k, log_norms, index_q, index_w, index_k, row_weight, offsets, key_map):
    key_rows = main_k.shape[0]
    own_rows, heads, index_width = index_q.shape
    main_heads = log_norms.shape[1]
    width = main_k.shape[1] // main_heads
    places_ctx = lax.axis_size("ctx")
    ranks = lax.axis_size("tp")
    here = lax.axis_index("ctx")
    rank = lax.axis_index("tp")
    far_bits = [b for b in (2**i for i in range(1, places_ctx.bit_length() - 1))]
    sums_of_bits = [sum(b for i, b in enumerate(far_bits) if n >> i & 1) for n in range(1, 2 ** len(far_bits))]
    near_far = [d for d in sums_of_bits if d & (d - 1) == 0]
    rest_far = sorted((d for d in sums_of_bits if d & (d - 1) != 0), key=int.bit_count)

    queries = prep(main_q, log_norms.T, width)
    keys_at = {0: main_k}
    for d in near_far:
        keys_at[d] = swap(main_k, d)
    keys_at[1] = swap(main_k, 1)
    index_w, row_weight, offsets, key_map, index_q, queries = together(
        index_w, row_weight, offsets, key_map, index_q, queries
    )
    far = [0] + near_far + rest_far
    order = far + [d + 1 for d in far]
    blocks = jnp.stack([here ^ d for d in order])
    places = jnp.concatenate([offsets[:1], rank.reshape(1), key_map[blocks] * key_rows]).astype(jnp.int32)

    def head_sums(members, parts):
        at = [(order.index(d), 0) for d in members]
        return mass(places, queries, at, [keys_at[d] for d in members], width, parts)

    def to_owners(sums):
        return [sums[0]] + [turn(sums[k], k) for k in range(1, ranks)]

    q_flat = index_q.reshape(own_rows * heads, index_width)
    row_weight = row_weight[:, None]
    tiles = own_rows // 8
    ends = [0, tiles * 2 // 7 * 8, tiles * 8]
    q_parts = [q_flat[a * heads : b * heads] for a, b in zip(ends, ends[1:])]
    w_parts = [index_w[a:b] for a, b in zip(ends, ends[1:])]
    firsts = []

    def index_part(n, index_keys, *others):
        rows = after(q_parts[n], *others)
        firsts.append(first_pass(places, (ends[n], own_rows), rows, index_keys, w_parts[n]))
        return firsts[-1][1]

    group_own = [0, 1]
    group_near = [d + side for d in near_far for side in (0, 1)]
    group_rest = [d + side for d in rest_far for side in (0, 1)]
    groups = [group_own, group_near, group_rest]
    columns = tuple((n, group.index(d)) for d in order for n, group in enumerate(groups) if d in group)

    sums_own = head_sums(group_own, 1)[0]
    index_k = after(index_k, sums_own)
    index_mine = [index_k] + [swap(index_k, d) for d in near_far + rest_far]
    got = together(*index_mine, *[keys_at[d] for d in near_far], row_weight, *q_parts, *w_parts)
    index_mine, got = got[: len(index_mine)], got[len(index_mine) :]
    keys_at.update(zip(near_far, got))
    row_weight, *got = got[len(near_far) :]
    q_parts, w_parts = got[: len(q_parts)], got[len(q_parts) :]
    index_theirs = swap(jnp.stack(index_mine), 1)
    sums_own = lax.psum_scatter(sums_own, "tp", scatter_dimension=0, tiled=True)
    for d in rest_far:
        lowest, highest = d & -d, 1 << (d.bit_length() - 1)
        source = jnp.where(here % 2 == 0, keys_at[d ^ lowest], keys_at[d ^ highest])
        keys_at[d] = lax.ppermute(
            source, "ctx", [(i, i ^ (highest if i % 2 else lowest)) for i in range(places_ctx)]
        )
    for d in near_far:
        keys_at[d + 1] = swap(keys_at[d], 1)
    index_keys = jnp.concatenate([*index_mine, index_theirs.reshape(-1, index_width)], axis=0)
    sums_near = head_sums(group_near, ranks)
    part_0 = index_part(0, index_keys, sums_near[0])
    sums_near = to_owners(sums_near)
    part_0, *got = together(part_0, *[keys_at[d] for d in rest_far])
    keys_at.update(zip(rest_far, got))
    for d in rest_far:
        keys_at[d + 1] = swap(keys_at[d], 1)
    sums_rest = head_sums(group_rest, ranks)
    index_part(1, index_keys, sums_rest[0])
    sums_rest = to_owners(sums_rest)
    grad_q, grad_w, mine, theirs = second_pass(
        firsts, [[sums_own], sums_near, sums_rest], columns, row_weight, index_w, index_keys, q_flat
    )

    mine = mine + swap(theirs, 1)
    terms = mine[:, :key_rows]
    for n, d in enumerate(far[1:], 1):
        terms = terms + swap(mine[:, n * key_rows : (n + 1) * key_rows], d)
    terms = terms.T.reshape(ranks, key_rows // ranks, index_width)
    grad_k = lax.dynamic_index_in_dim(terms, rank, 0, keepdims=False)
    for k in range(1, ranks):
        grad_k = grad_k + turn(lax.dynamic_index_in_dim(terms, (rank + k) % ranks, 0, keepdims=False), k)
    return (grad_q.reshape(index_q.shape), grad_w, grad_k)


def solution(mesh):
    placed = (
        P("ctx", "tp"),
        P("ctx", "tp"),
        P("ctx", "tp"),
        P(("ctx", "tp"), None, None),
        P(("ctx", "tp"), None),
        P("ctx", None),
        P(("ctx", "tp")),
        P("ctx"),
        P(),
    )
    return jax.shard_map(
        per_device,
        mesh=mesh,
        in_specs=placed,
        out_specs=(P(("ctx", "tp"), None, None), P(("ctx", "tp"), None), P(("ctx", "tp"), None)),
        check_vma=False,
    )
```

```python
import functools
import math

import jax
import jax.numpy as jnp
from jax import lax
from jax.experimental import pallas as pl
from jax.experimental.pallas import tpu as pltpu
from jax.sharding import PartitionSpec as P

LOG2E = math.log2(math.e)
LN2 = math.log(2.0)
TOP = 120.0
AHEAD = 5
VMEM_BYTES = 56 * 1024 * 1024
BF = jnp.bfloat16
F32 = jnp.float32


SHORT = pl.CostEstimate(flops=0, transcendentals=0, bytes_accessed=1024)


def prep_kernel(width, step_heads, root, q_ref, ln_ref, out_ref):
    heads, rows = ln_ref.shape
    pad, lanes = 256, 128
    cols = step_heads * lanes
    scaled = -root * ln_ref[...]
    high = scaled.astype(BF).astype(F32)
    mid = (scaled - high).astype(BF).astype(F32)
    low = (scaled - high - mid).astype(BF).astype(F32)
    terms = jnp.concatenate([high, mid, low], axis=0).astype(BF)
    column = lax.broadcasted_iota(jnp.int32, (3 * heads, cols), 1)
    source = lax.broadcasted_iota(jnp.int32, (3 * heads, cols), 0)
    head = source % heads - pl.program_id(0) * step_heads
    spare = jnp.where(head % 2 == 0, width - lanes, 0) + source // heads
    place = jnp.where(column == head * lanes + spare, 1.0, 0.0).astype(BF)
    extra = lax.dot_general(
        terms, place, (((0,), (0,)), ((), ())), preferred_element_type=F32
    ).astype(BF)
    lane = lax.broadcasted_iota(jnp.int32, (rows, lanes), 1)
    for h in range(step_heads):
        odd = h % 2
        first = (h // 2) * 2 * width + odd * (2 * width - pad)
        at = h * pad
        kept = lane >= pad - width if odd else lane < width - lanes
        mixed, plain = (0, lanes) if odd else (lanes, 0)
        out_ref[:, at + plain : at + plain + lanes] = q_ref[:, first + plain : first + plain + lanes]
        out_ref[:, at + mixed : at + mixed + lanes] = jnp.where(
            kept, q_ref[:, first + mixed : first + mixed + lanes], extra[:, h * lanes : (h + 1) * lanes]
        )


def prep(main_q, norms_turned, width, step_heads=8):
    rows = main_q.shape[0]
    heads = norms_turned.shape[0]
    return pl.pallas_call(
        functools.partial(prep_kernel, width, step_heads, math.sqrt(width)),
        grid=(heads // step_heads,),
        in_specs=[
            pl.BlockSpec((rows, step_heads * width), lambda i: (0, i)),
            pl.BlockSpec((heads, rows), lambda i: (0, 0)),
        ],
        out_specs=pl.BlockSpec((rows, step_heads * 256), lambda i: (0, i)),
        out_shape=jax.ShapeDtypeStruct((rows, heads * 256), BF),
        compiler_params=pltpu.CompilerParams(vmem_limit_bytes=VMEM_BYTES),
        cost_estimate=SHORT,
        name="prep",
    )(main_q, norms_turned)


def mass_kernel(width, step_heads, members, ranks, whole, pos_ref, qa_hbm, *refs):
    n_keys = len(members)
    key_hbm, out_refs = refs[:n_keys], refs[n_keys : n_keys + ranks]
    qa_ref, keys_ref, total_ref, q_sems, k_sems = refs[n_keys + ranks :]
    pad = 256
    factor = LOG2E / math.sqrt(width)
    rows, total = total_ref.shape
    steps = qa_ref.shape[1] // (step_heads * pad)
    copies = []
    for i in range(steps):
        cols = pl.ds(i * step_heads * pad, step_heads * pad)
        group = [pltpu.make_async_copy(qa_hbm.at[:, cols], qa_ref.at[:, cols], q_sems.at[i])]
        cols = pl.ds(i * step_heads * width, step_heads * width)
        first = 0
        for n, k in enumerate(key_hbm):
            at = pl.ds(first, k.shape[0])
            group.append(pltpu.make_async_copy(k.at[:, cols], keys_ref.at[at, cols], k_sems.at[i, n]))
            first += k.shape[0]
        copies.append(group)
    for group in copies[:2]:
        for copy in group:
            copy.start()
    lane = lax.broadcasted_iota(jnp.int32, (total, pad), 1)
    ones_even = jnp.where((lane >= width) & (lane < width + 3), 1.0, 0.0).astype(BF)
    ones_odd = jnp.where(lane < 3, 1.0, 0.0).astype(BF)
    keep_even = jnp.where(lane < width, 1.0, 0.0).astype(BF)
    keep_odd = jnp.where(lane >= pad - width, 1.0, 0.0).astype(BF)

    def one(h):
        first = (h // 2) * 2 * width + (h % 2) * (2 * width - pad)
        keys = keys_ref[:, first : first + pad]
        keys = keys * keep_odd + ones_odd if h % 2 else keys * keep_even + ones_even
        scores = lax.dot_general(
            qa_ref[:, h * pad : (h + 1) * pad], keys, (((1,), (1,)), ((), ())), preferred_element_type=F32
        )
        return jnp.exp2(scores * factor)

    for i in range(steps):
        for copy in copies[i]:
            copy.wait()
        for copy in copies[i + 2] if i + 2 < steps else []:
            copy.start()
        for h in range(i * step_heads, (i + 1) * step_heads, 2):
            both = one(h) + one(h + 1)
            total_ref[...] = both if h == 0 else total_ref[...] + both

    own = rows // ranks
    for k in range(ranks):
        first = 0 if whole else lax.rem(pos_ref[1] + k, ranks) * own
        column = 0
        for place, keys in zip(members, key_hbm):
            size = keys.shape[0]
            shape = (own, size)
            row = pos_ref[0] + first + lax.broadcasted_iota(jnp.int32, shape, 0)
            key = pos_ref[2 + place[0]] + place[1] + lax.broadcasted_iota(jnp.int32, shape, 1)
            mine = total_ref[tile_of(first, 1, own), column : column + size]
            out_refs[k][:, column : column + size] = jnp.where(key <= row, mine, 0.0)
            column += size


def mass(places, qa, members, key_list, width, ranks, step_heads=8):
    rows = qa.shape[0]
    heads = qa.shape[1] // 256
    total = sum(k.shape[0] for k in key_list)
    whole = ranks == 1
    hbm = pl.BlockSpec(memory_space=pltpu.HBM)
    own = rows // ranks
    steps = heads // step_heads
    vmem = pl.BlockSpec(memory_space=pltpu.VMEM)
    return pl.pallas_call(
        functools.partial(mass_kernel, width, step_heads, tuple(members), ranks, whole),
        in_specs=[pl.BlockSpec(memory_space=pltpu.SMEM), hbm] + [hbm] * len(key_list),
        out_specs=[vmem] * ranks,
        out_shape=[jax.ShapeDtypeStruct((own, total), F32)] * ranks,
        scratch_shapes=[
            pltpu.VMEM(qa.shape, BF),
            pltpu.VMEM((total, heads * width), BF),
            pltpu.VMEM((rows, total), F32),
            pltpu.SemaphoreType.DMA((steps,)),
            pltpu.SemaphoreType.DMA((steps, len(key_list))),
        ],
        compiler_params=pltpu.CompilerParams(vmem_limit_bytes=VMEM_BYTES),
        cost_estimate=SHORT,
        name="mass",
    )(places, qa, *key_list)


def in_pairs(steps, load, work, finish):
    pairs = (steps - 1) // 2
    load(0, 0)

    def two(p, _):
        first = 2 * p
        finish(first, 2)
        load(first + 1, 1)
        work(first, 0)
        load(first + 2, 0)
        work(first + 1, 1)
        return 0

    lax.fori_loop(0, pairs, two, 0)
    last = 2 * pairs
    if steps % 2 == 0:
        finish(last, 2)
        load(last + 1, 1)
        work(last, 0)
        work(last + 1, 1)
    else:
        finish(last, 1)
        work(last, 0)


def tile_of(i, step, size=None):
    size = step if size is None else size
    return pl.ds(i * step if isinstance(i, int) else pl.multiple_of(i * step, max(step, 8)), size)


def first_kernel(rows, scale, start, pos_ref, q_ref, key_ref, w_ref, power_hbm, prob_ref, most_ref, raw_0, raw_1, logits, ring, sems):
    keys = key_ref.shape[0]
    own, heads = w_ref.shape
    span = rows * heads
    steps = own // rows
    raws = (raw_0, raw_1)
    slots = ring.shape[0]

    def copy_out(i):
        slot = i % slots if isinstance(i, int) else lax.rem(i, slots)
        return pltpu.make_async_copy(ring.at[slot], power_hbm.at[tile_of(i, span), :], sems.at[slot])

    def multiply(i, slot):
        raws[slot][...] = lax.dot_general(
            q_ref[tile_of(i, span), :], key_ref[...], (((1,), (1,)), ((), ())), preferred_element_type=F32
        )

    def finish(i, count):
        for n in range(count):
            if isinstance(i, int):
                if i + n >= slots:
                    copy_out(i + n - slots).wait()
            else:

                @pl.when(i + n >= slots)
                def _():
                    copy_out(i + n - slots).wait()

    def elements(capped, i, slot):
        raw = raws[slot]
        where = i % slots if isinstance(i, int) else lax.rem(i, slots)
        w_turned = jnp.transpose(w_ref[tile_of(i, rows), :]) * LN2
        for t in range(rows):
            w = w_turned[:, t : t + 1]
            for c in range(keys // 128):
                at = (slice(t * heads, (t + 1) * heads), slice(c * 128, (c + 1) * 128))
                u = raw[at] * (scale * LOG2E)
                power = jnp.exp2(jnp.minimum(u, TOP) if capped else u)
                ring[(where, *at)] = power
                soft = jnp.log2(1.0 + power)
                soft = jnp.maximum(u, soft) if capped else soft
                logits[slot, t : t + 1, c * 128 : (c + 1) * 128] = jnp.sum(w * soft, axis=0, keepdims=True)
        prob_ref[tile_of(i, rows), :] = logits[slot]
        copy_out(i).start()

    q_most = jnp.zeros((8, 1), F32)
    for i in range(steps):
        part = jnp.sum(jnp.square(q_ref[tile_of(i, span), :].astype(F32)), axis=1, keepdims=True)
        q_most = jnp.maximum(q_most, jnp.max(part.reshape(-1, 8, 1), axis=0))
    k_most = jnp.max(jnp.sum(jnp.square(key_ref[...].astype(F32)), axis=1, keepdims=True))
    most_ref[...] = jnp.broadcast_to(q_most * (k_most * (scale * LOG2E) ** 2), most_ref.shape)
    past_top = jnp.max(most_ref[...]) > (TOP - 1.0) ** 2

    @pl.when(jnp.logical_not(past_top))
    def _():
        in_pairs(steps, multiply, functools.partial(elements, False), finish)

    @pl.when(past_top)
    def _():
        in_pairs(steps, multiply, functools.partial(elements, True), finish)

    blocks = pos_ref.shape[0] - 2
    size = keys // blocks
    row = pos_ref[0] + pos_ref[1] * start[1] + start[0] + lax.broadcasted_iota(jnp.int32, (own, size), 0)
    lane = lax.broadcasted_iota(jnp.int32, (own, size), 1)
    masked = jnp.concatenate(
        [
            jnp.where(pos_ref[2 + n] + lane <= row, prob_ref[:, n * size : (n + 1) * size], -jnp.inf)
            for n in range(blocks)
        ],
        axis=1,
    )
    top = jnp.max(masked, axis=1, keepdims=True)
    terms = jnp.exp2((masked - top) * LOG2E)
    prob_ref[...] = terms / jnp.sum(terms, axis=1, keepdims=True)
    for i in range(max(steps - slots, 0), steps):
        copy_out(i).wait()


def first_pass(places, start, q_flat, keys, weights, rows=8, slots=4):
    total, width = q_flat.shape
    key_total = keys.shape[0]
    own, heads = weights.shape
    tile = rows * heads
    vmem = pl.BlockSpec(memory_space=pltpu.VMEM)
    return pl.pallas_call(
        functools.partial(first_kernel, rows, 1.0 / math.sqrt(width), start),
        in_specs=[pl.BlockSpec(memory_space=pltpu.SMEM), vmem, vmem, vmem],
        out_specs=[pl.BlockSpec(memory_space=pltpu.HBM), vmem, vmem],
        out_shape=[
            jax.ShapeDtypeStruct((total, key_total), F32),
            jax.ShapeDtypeStruct((own, key_total), F32),
            jax.ShapeDtypeStruct((8, 128), F32),
        ],
        scratch_shapes=[
            pltpu.VMEM((tile, key_total), F32),
            pltpu.VMEM((tile, key_total), F32),
            pltpu.VMEM((2, rows, key_total), F32),
            pltpu.VMEM((slots, tile, key_total), F32),
            pltpu.SemaphoreType.DMA((slots,)),
        ],
        compiler_params=pltpu.CompilerParams(vmem_limit_bytes=VMEM_BYTES),
        cost_estimate=SHORT,
        name="first_pass",
    )(places, q_flat, keys, weights)


def second_kernel(rows, splits, cuts, columns, scale, rw_ref, w_ref, key_ref, q_ref, *refs):
    powers, probs, mosts, refs = refs[:cuts], refs[cuts : 2 * cuts], refs[2 * cuts : 3 * cuts], refs[3 * cuts :]
    count = sum(splits)
    parts, refs = refs[:count], refs[count:]
    gq_hbm, gw_ref, mine_ref, theirs_ref, power_ref, out_ref, coef_ref, grad_0, grad_1, sems, out_sems = refs
    grads = (grad_0, grad_1)
    keys = key_ref.shape[0]
    own, heads = w_ref.shape
    tile = rows * heads
    steps = own // rows
    lane = lax.broadcasted_iota(jnp.int32, (heads, 128), 1)

    def copy_in(i, source=powers[0], first=0):
        return pltpu.make_async_copy(source.at[tile_of(first, tile), :], power_ref.at[tile_of(i, tile), :], sems.at[i])

    def copy_out(i):
        at = tile_of(i, tile)
        return pltpu.make_async_copy(out_ref.at[at, :], gq_hbm.at[at, :], out_sems.at[i])

    sources = [(source, i) for source in powers for i in range(source.shape[0] // tile)]
    runs = [0]
    for source in powers:
        runs.append(runs[-1] + source.shape[0] // tile)

    def start_in(i):
        if isinstance(i, int):
            if i < steps:
                copy_in(i, *sources[i]).start()
        else:
            for source, low, high in zip(powers, runs, runs[1:]):

                @pl.when((i >= low) & (i < high))
                def _():
                    copy_in(i, source, i - low).start()

    for i in range(AHEAD):
        start_in(i)
    groups = []
    for size in splits:
        groups.append(sum(r[...] for r in parts[:size]))
        parts = parts[size:]
    span = keys // len(columns)
    mass_rows = jnp.concatenate([groups[g][:, n * span : (n + 1) * span] for g, n in columns], axis=1)
    target = mass_rows / jnp.sum(mass_rows, axis=1, keepdims=True)
    coef_ref[...] = rw_ref[...] * (jnp.concatenate([r[...] for r in probs], axis=0) - target)
    mine_ref[...] = jnp.zeros_like(mine_ref)
    theirs_ref[...] = jnp.zeros_like(theirs_ref)
    side = keys // 2

    def add_column(block, t, values):
        return jnp.where(lane == t, jnp.sum(values, axis=1, keepdims=True), block)

    def as_rows(block):
        return jnp.transpose(block)[:rows, :] * LN2

    def elements(i, slot):
        coef = coef_ref[tile_of(i, rows), :]
        w_turned = jnp.transpose(w_ref[tile_of(i, rows), :]) * scale
        block = jnp.zeros((heads, 128), F32)
        for t in range(rows):
            w = w_turned[:, t : t + 1]
            total = jnp.zeros((heads, 128), F32)
            from_row = tile_of(i * rows + t, heads)
            for c in range(keys // 128):
                cols = slice(c * 128, (c + 1) * 128)
                row = coef[t : t + 1, cols]
                power = power_ref[from_row, cols]
                up = 1.0 + power
                grads[slot][t * heads : (t + 1) * heads, cols] = (
                    power * pl.reciprocal(up, approx=False) * (row * w)
                ).astype(BF)
                total = total + jnp.log2(up) * row
            block = add_column(block, t, total)
        gw_ref[tile_of(i, rows), :] = as_rows(block)

    def multiply(i, slot):
        block = grads[slot][...]
        at = tile_of(i, tile)
        out_ref[at, :] = jnp.dot(block, key_ref[...], preferred_element_type=F32)
        turned = jnp.transpose(q_ref[at, :])
        mine_ref[...] += jnp.dot(turned, block[:, :side], preferred_element_type=F32)
        theirs_ref[...] += jnp.dot(turned, block[:, side:], preferred_element_type=F32)
        copy_out(i).start()

    def finish(i, number):
        for n in range(1, number + 1):
            if not isinstance(i, int) or i + n < steps:
                copy_in(i + n).wait()
        for n in range(1, number + 1):
            start_in(i + AHEAD - 1 + n)

    copy_in(0).wait()
    in_pairs(steps, elements, multiply, finish)
    most = functools.reduce(jnp.maximum, [r[...] for r in mosts])

    @pl.when(jnp.max(most) > (TOP - 1.0) ** 2)
    def _():
        def past_top(i, _):
            raw = lax.dot_general(
                q_ref[tile_of(i, tile), :], key_ref[...], (((1,), (1,)), ((), ())), preferred_element_type=F32
            )
            over = jnp.maximum(raw * (scale * LOG2E) - TOP, 0.0)
            coef = coef_ref[tile_of(i, rows), :]
            block = jnp.zeros((heads, 128), F32)
            for t in range(rows):
                block = add_column(block, t, over[t * heads : (t + 1) * heads, :] * coef[t : t + 1, :])
            gw_ref[tile_of(i, rows), :] += as_rows(block)
            return 0

        lax.fori_loop(0, steps, past_top, 0)

    for i in range(steps):
        copy_out(i).wait()


def second_pass(firsts, mass_parts, columns, row_weight, weights, keys, q_flat, rows=8):
    powers, probs, mosts = zip(*firsts)
    key_total = keys.shape[0]
    total = q_flat.shape[0]
    own, heads = weights.shape
    tile = rows * heads
    steps = own // rows
    width = keys.shape[1]
    flat = [piece for pieces in mass_parts for piece in pieces]
    vmem = pl.BlockSpec(memory_space=pltpu.VMEM)
    hbm = pl.BlockSpec(memory_space=pltpu.HBM)
    return pl.pallas_call(
        functools.partial(
            second_kernel,
            rows,
            tuple(len(p) for p in mass_parts),
            len(powers),
            columns,
            1.0 / math.sqrt(width),
        ),
        in_specs=[vmem] * 4 + [hbm] * len(powers) + [vmem] * (2 * len(probs) + len(flat)),
        out_specs=[hbm, vmem, vmem, vmem],
        out_shape=[
            jax.ShapeDtypeStruct((total, width), F32),
            jax.ShapeDtypeStruct((own, heads), F32),
            jax.ShapeDtypeStruct((width, key_total // 2), F32),
            jax.ShapeDtypeStruct((width, key_total // 2), F32),
        ],
        scratch_shapes=[
            pltpu.VMEM((total, key_total), F32),
            pltpu.VMEM((total, width), F32),
            pltpu.VMEM((own, key_total), F32),
            pltpu.VMEM((tile, key_total), BF),
            pltpu.VMEM((tile, key_total), BF),
            pltpu.SemaphoreType.DMA((steps,)),
            pltpu.SemaphoreType.DMA((steps,)),
        ],
        compiler_params=pltpu.CompilerParams(vmem_limit_bytes=VMEM_BYTES),
        cost_estimate=SHORT,
        name="second_pass",
    )(row_weight, weights, keys, q_flat, *powers, *probs, *mosts, *flat)


def swap(x, bit):
    size = lax.axis_size("ctx")
    return lax.ppermute(x, "ctx", [(i, i ^ bit) for i in range(size)])


def turn(x, steps):
    size = lax.axis_size("tp")
    return lax.ppermute(x, "tp", [(i, (i + steps) % size) for i in range(size)])


def together(*values):
    return lax.optimization_barrier(values)


def after(x, *others):
    return lax.optimization_barrier((x, *others))[0]


def per_device(main_q, main_k, log_norms, index_q, index_w, index_k, row_weight, offsets, key_map):
    key_rows = main_k.shape[0]
    own_rows, heads, index_width = index_q.shape
    main_heads = log_norms.shape[1]
    width = main_k.shape[1] // main_heads
    places_ctx = lax.axis_size("ctx")
    ranks = lax.axis_size("tp")
    here = lax.axis_index("ctx")
    rank = lax.axis_index("tp")
    far_bits = [b for b in (2**i for i in range(1, places_ctx.bit_length() - 1))]
    sums_of_bits = [sum(b for i, b in enumerate(far_bits) if n >> i & 1) for n in range(1, 2 ** len(far_bits))]
    near_far = [d for d in sums_of_bits if d & (d - 1) == 0]
    rest_far = sorted((d for d in sums_of_bits if d & (d - 1) != 0), key=int.bit_count)

    queries = prep(main_q, log_norms.T, width)
    keys_at = {0: main_k}
    for d in near_far:
        keys_at[d] = swap(main_k, d)
    keys_at[1] = swap(main_k, 1)
    index_w, row_weight, offsets, key_map, index_q, queries = together(
        index_w, row_weight, offsets, key_map, index_q, queries
    )
    far = [0] + near_far + rest_far
    order = far + [d + 1 for d in far]
    blocks = jnp.stack([here ^ d for d in order])
    places = jnp.concatenate([offsets[:1], rank.reshape(1), key_map[blocks] * key_rows]).astype(jnp.int32)

    def head_sums(members, parts):
        at = [(order.index(d), 0) for d in members]
        return mass(places, queries, at, [keys_at[d] for d in members], width, parts)

    def to_owners(sums):
        return [sums[0]] + [turn(sums[k], k) for k in range(1, ranks)]

    q_flat = index_q.reshape(own_rows * heads, index_width)
    row_weight = row_weight[:, None]
    tiles = own_rows // 8
    ends = [0, tiles * 2 // 7 * 8, tiles * 8]
    q_parts = [q_flat[a * heads : b * heads] for a, b in zip(ends, ends[1:])]
    w_parts = [index_w[a:b] for a, b in zip(ends, ends[1:])]
    firsts = []

    def index_part(n, index_keys, *others):
        rows = after(q_parts[n], *others)
        firsts.append(first_pass(places, (ends[n], own_rows), rows, index_keys, w_parts[n]))
        return firsts[-1][1]

    group_own = [0, 1]
    group_near = [d + side for d in near_far for side in (0, 1)]
    group_rest = [d + side for d in rest_far for side in (0, 1)]
    groups = [group_own, group_near, group_rest]
    columns = tuple((n, group.index(d)) for d in order for n, group in enumerate(groups) if d in group)

    sums_own = head_sums(group_own, 1)[0]
    index_k = after(index_k, sums_own)
    index_mine = [index_k] + [swap(index_k, d) for d in near_far + rest_far]
    sums_own = lax.psum_scatter(sums_own, "tp", scatter_dimension=0, tiled=True)
    sums_own, *got = together(
        sums_own, *index_mine, *[keys_at[d] for d in near_far], row_weight, *q_parts, *w_parts
    )
    index_mine, got = got[: len(index_mine)], got[len(index_mine) :]
    keys_at.update(zip(near_far, got))
    row_weight, *got = got[len(near_far) :]
    q_parts, w_parts = got[: len(q_parts)], got[len(q_parts) :]
    index_theirs = swap(jnp.stack(index_mine), 1)
    for d in rest_far:
        lowest, highest = d & -d, 1 << (d.bit_length() - 1)
        source = jnp.where(here % 2 == 0, keys_at[d ^ lowest], keys_at[d ^ highest])
        keys_at[d] = lax.ppermute(
            source, "ctx", [(i, i ^ (highest if i % 2 else lowest)) for i in range(places_ctx)]
        )
    for d in near_far:
        keys_at[d + 1] = swap(keys_at[d], 1)
    index_keys = jnp.concatenate([*index_mine, index_theirs.reshape(-1, index_width)], axis=0)
    sums_near = head_sums(group_near, 1)
    part_0 = index_part(0, index_keys, sums_near[0])
    sums_near = [lax.psum_scatter(sums_near[0], "tp", scatter_dimension=0, tiled=True)]
    part_0, *got = together(part_0, *[keys_at[d] for d in rest_far])
    keys_at.update(zip(rest_far, got))
    for d in rest_far:
        keys_at[d + 1] = swap(keys_at[d], 1)
    sums_rest = head_sums(group_rest, ranks)
    index_part(1, index_keys, sums_rest[0])
    sums_rest = to_owners(sums_rest)
    grad_q, grad_w, mine, theirs = second_pass(
        firsts, [[sums_own], sums_near, sums_rest], columns, row_weight, index_w, index_keys, q_flat
    )

    mine = mine + swap(theirs, 1)
    terms = mine[:, :key_rows]
    for n, d in enumerate(far[1:], 1):
        terms = terms + swap(mine[:, n * key_rows : (n + 1) * key_rows], d)
    terms = terms.T.reshape(ranks, key_rows // ranks, index_width)
    grad_k = lax.dynamic_index_in_dim(terms, rank, 0, keepdims=False)
    for k in range(1, ranks):
        grad_k = grad_k + turn(lax.dynamic_index_in_dim(terms, (rank + k) % ranks, 0, keepdims=False), k)
    return (grad_q.reshape(index_q.shape), grad_w, grad_k)


def solution(mesh):
    placed = (
        P("ctx", "tp"),
        P("ctx", "tp"),
        P("ctx", "tp"),
        P(("ctx", "tp"), None, None),
        P(("ctx", "tp"), None),
        P("ctx", None),
        P(("ctx", "tp")),
        P("ctx"),
        P(),
    )
    return jax.shard_map(
        per_device,
        mesh=mesh,
        in_specs=placed,
        out_specs=(P(("ctx", "tp"), None, None), P(("ctx", "tp"), None), P(("ctx", "tp"), None)),
        check_vma=False,
    )
```
